32 devices in a mesh: blk: 8 (over y, x, core), tp: 4 (over z).
Axes of the slice: x: 2, y: 2, z: 4, core: 2. Of those that a mesh axis runs over, the one named last changes fastest.
Arguments:
- hidden_in: bfloat16 [4096, 6144], P('blk', 'tp'), may hold values from -40 to 40
- ln_gain: float32 [6144], replicated, may hold values from 0.1 to 1.9
- w_qkv: bfloat16 [6144, 3, 3072], P(None, None, 'tp'), may hold values from -1 to 1
- w_out: bfloat16 [3072, 6144], P('tp'), may hold values from -0.625 to 0.625
- doc_lengths: int32 [32], replicated, may hold values from 0 to 2048, as said below
- segment_ids: int32 [4096], P('blk'), may hold values from 0 to 31, as said below
- pair_table: int32 [8, 8], replicated, may hold values from 0 to 1, as said below
- page_table: int32 [256], P('blk'), may hold values from 0 to 255, as said below
Outputs:
- attn_out: bfloat16 [4096, 6144], P('blk', 'tp')
- page_cache: bfloat16 [2, 256, 16, 3072], P(None, 'blk', None, 'tp')
The draws below stay inside these ranges and needn't reach their ends.
Inputs may be any that keep to these rules, and one draw needn't show every extreme that they name: `doc_lengths`: the 32 documents in stream order; they sum to 4096, the empty ones stand just before the last slot, which holds the stream's last document, and the second document has exactly 2048 tokens. segment_ids[t] is the number of documents that end at or before token t; the last token belongs to slot 31. pair_table[i, j] is 1 exactly where a token of block j of 512 tokens and a token at or after it in block i lie in one document. `page_table`: the 32 entries of one block of tokens are that block's own page numbers, each once.
All inputs are finite; a program needn't handle non-finite values.
Results may differ from the reference program's by a relative error of at most 0.014.
Values may be sent and summed in bfloat16 or wider, within the bound.
No kernel may reach another device: no remote copies, remote signals or barrier semaphores. Data moves between devices by JAX's collectives and lax.ppermute only.
A program may use at most 256 MiB of HBM per device.

```python
import jax
import jax.numpy as jnp
from jax import lax

D = 6144
HEADS = 32
HD = 96
ROT = 24
PAGE = 16
TOK_DEV = 512
TOKENS = 4096
MOST = 2048
NDOCS = 32
NPAGES = 256
PG_DEV = 32
N_BLK = 8
N_TP = 4


def document_ends(key):
    base = jax.random.fold_in(key, 17)
    key_rest, key_first = jax.random.split(base)
    rest = jax.random.randint(key_rest, (NDOCS,), TOK_DEV // 4, MOST + 1, dtype=jnp.int32)
    opening_len = jax.random.randint(key_first, (), TOK_DEV // 4, MOST - TOK_DEV + 1, dtype=jnp.int32)
    opening_len = opening_len + (opening_len % TOK_DEV == 0).astype(jnp.int32)
    raw_lengths = rest.at[0].set(opening_len).at[1].set(MOST)
    capped = jnp.minimum(jnp.cumsum(raw_lengths), TOKENS).astype(jnp.int32)
    below = capped < TOKENS
    last_start = jnp.max(jnp.where(below, capped, 0)).astype(jnp.int32)
    shifted = jnp.where(below, capped, last_start).astype(jnp.int32)
    return shifted.at[NDOCS - 1].set(TOKENS).astype(jnp.int32)


def segment_numbers(key):
    doc_ends = document_ends(key)
    token_index = jnp.arange(TOKENS, dtype=jnp.int32)
    return jnp.sum((doc_ends[None, :] <= token_index[:, None]).astype(jnp.int32), axis=1).astype(jnp.int32)


def draw_doc_lengths(key, part):
    doc_ends = document_ends(key)
    earlier = jnp.concatenate([jnp.zeros((1,), jnp.int32), doc_ends[:-1]])
    return (doc_ends - earlier).astype(jnp.int32)


def draw_segment_ids(key, part):
    return segment_numbers(key)


def draw_pair_table(key, part):
    segments = segment_numbers(key)
    block_total = TOKENS // TOK_DEV
    opening = segments[::TOK_DEV]
    closing = segments[TOK_DEV - 1::TOK_DEV]
    row_ids = jnp.arange(block_total, dtype=jnp.int32)[:, None]
    col_ids = jnp.arange(block_total, dtype=jnp.int32)[None, :]
    table = (row_ids == col_ids) | (col_ids < row_ids) & (closing[None, :] == opening[:, None])
    return table.astype(jnp.int32)


def draw_page_table(key, part):
    block_total = TOKENS // TOK_DEV
    block_keys = jax.random.split(jax.random.fold_in(key, 29), block_total)
    orders = jax.vmap(lambda single: jax.random.permutation(single, PG_DEV))(block_keys).astype(jnp.int32)
    offsets = (jnp.arange(block_total, dtype=jnp.int32) * PG_DEV)[:, None]
    return (orders + offsets).reshape(NPAGES).astype(jnp.int32)


def draw_hidden_in(key, part):
    key_one = jax.random.fold_in(key, 0)
    result = jnp.clip(jax.random.normal(key_one, (TOKENS, D), jnp.float32), -6.0, 6.0)
    return result.astype(jnp.bfloat16)


def draw_w_qkv(key, part):
    key_one = jax.random.fold_in(key, 0)
    scale = D ** (-0.5)
    result = jnp.clip(jax.random.normal(key_one, (D, 3, HEADS * HD), jnp.float32), -6.0, 6.0) * scale
    return result.astype(jnp.bfloat16)


def spiked(drawn, own_key, source, target, shards_of, factor):
    owner, partner = [(jnp.arange(drawn.shape[axis_at]) // (drawn.shape[axis_at] // shards_of)).reshape([-1 if axis == axis_at else 1 for axis in range(drawn.ndim)]) for axis_at in (source, target)]
    chosen = jax.random.permutation(own_key, shards_of)[partner]
    strong = (owner == chosen) | (owner == (partner + shards_of // 2) % shards_of)
    return jnp.where(strong, factor * drawn, drawn)


def steps_of(key, extent, cuts, low, largest):
    def one(position, shards_of):
        heights = jax.random.uniform(jax.random.fold_in(jax.random.fold_in(key, 6), position), (shards_of,), jnp.float32, low / len(cuts), largest / len(cuts))
        return jnp.repeat(jnp.exp(heights), extent[position] // shards_of).reshape((-1,) + (1,) * (len(extent) - position - 1))

    factor_of = one(*cuts[0])
    for cut in cuts[1:]:
        factor_of = factor_of * one(*cut)
    return factor_of


def noise_with(own_key, extent, spread, most, cuts, heavy, kind=jnp.bfloat16):
    values = spread * jax.random.normal(own_key, extent, jnp.float32)
    if cuts:
        values = values * steps_of(own_key, extent, cuts, -0.22, 0.18)
    return jnp.clip(spiked(values, jax.random.fold_in(own_key, 3), *heavy), -most, most).astype(kind)


def setup_inputs(seed: int = 0) -> dict:
    splits = jax.random.split(jax.random.key(seed), 9)
    return {
        "hidden_in": draw_hidden_in(jax.random.fold_in(splits[8], 71), 0),
        "ln_gain": jnp.clip(1.0 + 0.18 * jax.random.normal(splits[1], (D,), jnp.float32), 0.1, 1.9),
        "w_qkv": draw_w_qkv(jax.random.fold_in(splits[8], 71), 0),
        "w_out": noise_with(splits[3], (HEADS * HD, D), (HEADS * HD // 16) ** -0.5, 0.625, ((0, 4),), (0, 1, 4, 2.0)),
        "doc_lengths": draw_doc_lengths(jax.random.fold_in(splits[8], 71), 0),
        "segment_ids": draw_segment_ids(jax.random.fold_in(splits[8], 71), 0),
        "pair_table": draw_pair_table(jax.random.fold_in(splits[8], 71), 0),
        "page_table": draw_page_table(jax.random.fold_in(splits[8], 71), 0),
    }


EPSILON = 1e-05

def layer_norm(hidden_in, ln_gain):
    values32 = hidden_in.astype(jnp.float32)
    row_mean = lax.optimization_barrier(jnp.mean(values32, axis=-1, keepdims=True))
    centred = values32 - row_mean
    row_var = lax.optimization_barrier(jnp.mean(centred * centred, axis=-1, keepdims=True))
    return (centred * lax.rsqrt(row_var + EPSILON) * ln_gain).astype(jnp.bfloat16)

def doc_positions(token_index, doc_lengths, segment_ids):
    starts = (jnp.cumsum(doc_lengths) - doc_lengths).astype(jnp.int32)
    slots = jnp.arange(doc_lengths.shape[0], dtype=jnp.int32)
    in_document = segment_ids[:, None] == slots[None, :]
    offsets = lax.optimization_barrier(jnp.sum(jnp.where(in_document, starts[None, :], 0), axis=1)).astype(jnp.int32)
    return (token_index - offsets).astype(jnp.int32)

def rotary(head_block, positions):
    half_rot = ROT // 2
    frequency = 10000.0 ** (-(2.0 * jnp.arange(half_rot, dtype=jnp.float32)) / ROT)
    angles = positions.astype(jnp.float32)[:, None] * frequency[None, :]
    cosine = jnp.cos(angles)[:, None, :]
    sine_part = jnp.sin(angles)[:, None, :]
    lower_half = head_block[..., :half_rot]
    upper_half = head_block[..., half_rot:ROT]
    return jnp.concatenate([lower_half * cosine - upper_half * sine_part, upper_half * cosine + lower_half * sine_part, head_block[..., ROT:]], axis=-1)

def attention(queries, key_rows, values, segment_ids, pair_table):
    reach = N_BLK // 2
    window = (reach + 1) * TOK_DEV
    scale = HD ** (-0.5)

    def one_block(block_id):
        q_start = block_id * TOK_DEV
        k_start = jnp.maximum(block_id - reach, 0) * TOK_DEV
        q_part = lax.dynamic_slice_in_dim(queries, q_start, TOK_DEV, 0).astype(jnp.float32)
        k_part = lax.dynamic_slice_in_dim(key_rows, k_start, window, 0).astype(jnp.float32)
        v_part = lax.dynamic_slice_in_dim(values, k_start, window, 0).astype(jnp.float32)
        q_seg = lax.dynamic_slice_in_dim(segment_ids, q_start, TOK_DEV, 0)
        k_seg = lax.dynamic_slice_in_dim(segment_ids, k_start, window, 0)
        q_index = q_start + jnp.arange(TOK_DEV, dtype=jnp.int32)
        k_index = k_start + jnp.arange(window, dtype=jnp.int32)
        table_row = lax.dynamic_index_in_dim(pair_table, block_id, 0, keepdims=False)
        live = jnp.take(table_row, k_index // TOK_DEV)
        allowed = (live[None, :] > 0) & (q_seg[:, None] == k_seg[None, :]) & (k_index[None, :] <= q_index[:, None])
        scores = jnp.einsum('qhd,khd->hqk', q_part, k_part) * scale
        scores = jnp.where(allowed[None], scores, -jnp.inf)
        peak = lax.optimization_barrier(jnp.max(scores, axis=-1, keepdims=True))
        weights = jnp.exp(scores - peak)
        totals = lax.optimization_barrier(jnp.sum(weights, axis=-1))
        rounded = lax.optimization_barrier(weights.astype(jnp.bfloat16)).astype(jnp.float32)
        mixed = jnp.einsum('hqk,khd->qhd', rounded, v_part) / jnp.transpose(totals)[:, :, None]
        return mixed.astype(jnp.bfloat16)
    blocks = lax.map(one_block, jnp.arange(N_BLK, dtype=jnp.int32))
    return blocks.reshape(TOKENS, HEADS * HD)

def reference(hidden_in, ln_gain, w_qkv, w_out, doc_lengths, segment_ids, pair_table, page_table):
    normed = layer_norm(hidden_in, ln_gain)
    projected = jnp.dot(normed, w_qkv.reshape(D, 3 * HEADS * HD), preferred_element_type=jnp.float32).reshape(TOKENS, 3, HEADS, HD)
    token_index = jnp.arange(TOKENS, dtype=jnp.int32)
    positions = doc_positions(token_index, doc_lengths, segment_ids)
    queries = rotary(projected[:, 0], positions).astype(jnp.bfloat16)
    key_rows = rotary(projected[:, 1], positions).astype(jnp.bfloat16)
    values = projected[:, 2].astype(jnp.bfloat16)
    heads_out = attention(queries, key_rows, values, segment_ids, pair_table)
    group_cols = HEADS * HD // N_TP
    summed = jnp.zeros((TOKENS, D), jnp.float32)
    for group_id in range(N_TP):
        partial_term = jnp.dot(heads_out[:, group_id * group_cols:(group_id + 1) * group_cols], w_out[group_id * group_cols:(group_id + 1) * group_cols], preferred_element_type=jnp.float32)
        summed = summed + lax.optimization_barrier(partial_term.astype(jnp.bfloat16)).astype(jnp.float32)
    attn_out = summed.astype(jnp.bfloat16)
    stacked = jnp.stack([key_rows.reshape(NPAGES, PAGE, HEADS * HD), values.reshape(NPAGES, PAGE, HEADS * HD)])
    page_cache = jnp.zeros_like(stacked).at[:, page_table].set(stacked)
    return (attn_out, page_cache)
```

```python
import functools

import jax
import jax.numpy as jnp
from jax import lax
from jax.experimental import pallas as pl
from jax.experimental.pallas import tpu as pltpu
from jax.sharding import PartitionSpec as P

HD = 96
ROT = 24
PAGE = 16


EPSILON = 1e-05
CHUNKS = 2


def from_behind(value, axis, steps):
    count = lax.axis_size(axis)
    first, last = (max(0, -steps), min(count, count - steps))
    return lax.ppermute(value, axis, [(source, source + steps) for source in range(first, last)])


def layer_norm(whole, ln_gain):
    values32 = whole.astype(jnp.float32)
    row_mean = jnp.mean(values32, axis=-1, keepdims=True)
    centred = values32 - row_mean
    row_var = jnp.mean(centred * centred, axis=-1, keepdims=True)
    return (centred * lax.rsqrt(row_var + EPSILON) * ln_gain).astype(jnp.bfloat16)


def doc_positions(token_index, doc_lengths, segment_ids):
    starts = jnp.cumsum(doc_lengths) - doc_lengths
    slots = jnp.arange(doc_lengths.shape[0], dtype=jnp.int32)
    in_document = segment_ids[:, None] == slots[None, :]
    offsets = jnp.sum(jnp.where(in_document, starts[None, :], 0), axis=1)
    return token_index - offsets


def rotary(head_block, positions):
    half_rot = ROT // 2
    frequency = 10000.0 ** (-(2.0 * jnp.arange(half_rot, dtype=jnp.float32)) / ROT)
    angles = positions.astype(jnp.float32)[:, None] * frequency[None, :]
    cosine = jnp.cos(angles)[:, None, :]
    sine_part = jnp.sin(angles)[:, None, :]
    lower_half = head_block[..., :half_rot]
    upper_half = head_block[..., half_rot:ROT]
    return jnp.concatenate(
        [
            lower_half * cosine - upper_half * sine_part,
            upper_half * cosine + lower_half * sine_part,
            head_block[..., ROT:],
        ],
        axis=-1,
    )


def per_device_any(hidden_in, ln_gain, w_qkv, w_out, doc_lengths, segment_ids, pair_table, page_table):
    row_count = hidden_in.shape[0]
    whole = lax.all_gather(hidden_in, "tp", axis=1, tiled=True)
    normed = layer_norm(whole, ln_gain)
    col_count = w_qkv.shape[2]
    head_count = col_count // HD
    projected = jnp.einsum("tk,kcn->ctn", normed, w_qkv, preferred_element_type=jnp.float32)
    projected = projected.reshape(3, row_count, head_count, HD)
    block_index = lax.axis_index("blk")
    token_index = block_index * row_count + jnp.arange(row_count, dtype=jnp.int32)
    positions = doc_positions(token_index, doc_lengths, segment_ids)
    queries = rotary(projected[0], positions).astype(jnp.bfloat16)
    key_rows = rotary(projected[1], positions).astype(jnp.bfloat16)
    values = projected[2].astype(jnp.bfloat16)
    table_row = lax.dynamic_index_in_dim(pair_table, block_index, 0, keepdims=False)
    block_ids = jnp.arange(pair_table.shape[1], dtype=jnp.int32)
    scale = HD ** (-0.5)

    def attend(running, incoming, offset):
        key_piece, value_piece, segment_piece = incoming
        piece_rows = key_piece.shape[0]
        key_index = offset + jnp.arange(piece_rows, dtype=jnp.int32)
        matches = (key_index // row_count)[:, None] == block_ids[None, :]
        live = jnp.sum(jnp.where(matches, table_row[None, :], 0), axis=1) > 0

        def compute(previous):
            maxima, totals, weighted = previous
            scores = (
                jnp.einsum("qhd,khd->hqk", queries, key_piece, preferred_element_type=jnp.float32)
                * scale
            )
            allowed = (
                live[None, :]
                & (segment_ids[:, None] == segment_piece[None, :])
                & (key_index[None, :] <= token_index[:, None])
            )
            scores = jnp.where(allowed[None], scores, -jnp.inf)
            newest = jnp.maximum(maxima, jnp.max(scores, axis=-1))
            shrink = jnp.exp(maxima - newest)
            weights = jnp.exp(scores - newest[..., None])
            totals = totals * shrink + jnp.sum(weights, axis=-1)
            weighted = weighted * shrink[..., None] + jnp.einsum(
                "hqk,khd->hqd",
                weights.astype(jnp.bfloat16),
                value_piece,
                preferred_element_type=jnp.float32,
            )
            return (newest, totals, weighted)

        return lax.cond(jnp.any(live), compute, lambda previous: previous, running)

    start_state = (
        jnp.full((head_count, row_count), -1e30, jnp.float32),
        jnp.zeros((head_count, row_count), jnp.float32),
        jnp.zeros((head_count, row_count, HD), jnp.float32),
    )
    final = attend(start_state, (key_rows, values, segment_ids), block_index * row_count)
    for distance in range(1, lax.axis_size("blk") // 2 + 1):
        earlier = from_behind((key_rows, values, segment_ids), "blk", distance)
        final = attend(final, earlier, (block_index - distance) * row_count)
    mixed = (final[2] / final[1][..., None]).astype(jnp.bfloat16)
    heads_out = jnp.transpose(mixed, (1, 0, 2)).reshape(row_count, col_count)
    partial_term = jnp.dot(heads_out, w_out, preferred_element_type=jnp.float32)
    attn_out = lax.psum_scatter(
        partial_term.astype(jnp.bfloat16), "tp", scatter_dimension=1, tiled=True
    )
    page_count = row_count // PAGE
    local_pages = page_table - block_index * page_count
    stacked = jnp.stack(
        [key_rows.reshape(page_count, PAGE, col_count), values.reshape(page_count, PAGE, col_count)]
    )
    page_cache = jnp.zeros_like(stacked).at[:, local_pages].set(stacked)
    return (attn_out, page_cache)


def line_gather(value):
    place = lax.axis_index("tp")
    up1 = lax.ppermute(value, "tp", [(0, 1), (1, 2), (2, 3)])
    down1 = lax.ppermute(value, "tp", [(3, 2), (2, 1), (1, 0)])
    up2 = lax.ppermute(up1, "tp", [(1, 2), (2, 3)])
    down2 = lax.ppermute(down1, "tp", [(2, 1), (1, 0)])
    inner = jnp.where(place == 2, up2, down2)
    outer = lax.ppermute(inner, "tp", [(2, 3), (1, 0)])
    first = jnp.where(place == 0, down1, up1)
    second = jnp.where(place == 0, down2, jnp.where(place == 3, up2, down1))
    third = jnp.where((place == 0) | (place == 3), outer, inner)
    return [first, second, third]


def line_owners():
    place = lax.axis_index("tp")
    first = jnp.where(place == 0, 1, place - 1)
    second = jnp.where(place == 0, 2, jnp.where(place == 3, 1, place + 1))
    third = jnp.where(place < 2, 3, 0)
    return [place, first, second, third]


def norm_into(x_ref, mean_ref, rstd_ref, gain_ref, normed_ref):
    centred = x_ref[...].astype(jnp.float32) - mean_ref[...]
    normed_ref[...] = (centred * rstd_ref[...] * gain_ref[0]).astype(jnp.bfloat16)


def project_kernel(has_previous, is_last, owner_ref, *refs):
    refs = list(refs)
    x_ref, mean_ref, rstd_ref, gain_ref, w_ref = refs[:5]
    del refs[:5]
    previous_ref = refs.pop(0) if has_previous else None
    cos_ref, sin_ref = (refs.pop(0), refs.pop(0)) if is_last else (None, None)
    out_ref, normed_ref = refs
    step = pl.program_id(0)

    @pl.when(step == 0)
    def _():
        norm_into(x_ref, mean_ref, rstd_ref, gain_ref, normed_ref)

    product = jnp.dot(normed_ref[...], w_ref[0], preferred_element_type=jnp.float32)
    if has_previous:
        product = product + previous_ref[0]
    if not is_last:
        out_ref[0] = product
        return
    turned = product.T
    group = turned.shape[0] // HD
    out_ref[...] = turned.reshape(group, HD, turned.shape[1]).astype(jnp.bfloat16)

    @pl.when(step < 4)
    def _():
        half = ROT // 2
        for head in range(group):
            part = turned[head * HD : head * HD + ROT]
            swapped = jnp.concatenate([part[half:], part[:half]], axis=0)
            out_ref[head, :ROT] = (part * cos_ref[...] + swapped * sin_ref[...]).astype(jnp.bfloat16)


def project(owner, x, mean, rstd, gain, w3, previous=None, tables=None):
    rows, depth = x.shape
    width = w3.shape[2]
    half = width // 2
    is_last = tables is not None
    in_specs = [
        pl.BlockSpec((rows, depth), lambda s, o: (0, 0)),
        pl.BlockSpec((rows, 1), lambda s, o: (0, 0)),
        pl.BlockSpec((rows, 1), lambda s, o: (0, 0)),
        pl.BlockSpec((1, 1, depth), lambda s, o: (o[0], 0, 0)),
        pl.BlockSpec((1, depth, half), lambda s, o: (s // 2, o[0], s % 2)),
    ]
    args = [x, mean, rstd, gain, w3]
    sums = pl.BlockSpec((1, rows, half), lambda s, o: (s // 2, 0, s % 2))
    if previous is not None:
        in_specs.append(sums)
        args.append(previous)
    if is_last:
        in_specs += [pl.BlockSpec((ROT, rows), lambda s, o: (0, 0))] * 2
        args += list(tables)
        heads = width // HD
        out_shape = jax.ShapeDtypeStruct((heads, 3 * HD, rows), jnp.bfloat16)
        out_spec = pl.BlockSpec((heads // 2, HD, rows), lambda s, o: (s % 2, s // 2, 0))
    else:
        out_shape = jax.ShapeDtypeStruct((3, rows, width), jnp.float32)
        out_spec = sums
    return pl.pallas_call(
        functools.partial(project_kernel, previous is not None, is_last),
        grid_spec=pltpu.PrefetchScalarGridSpec(
            num_scalar_prefetch=1,
            grid=(6,),
            in_specs=in_specs,
            out_specs=out_spec,
            scratch_shapes=[pltpu.VMEM((rows, depth), jnp.bfloat16)],
        ),
        out_shape=out_shape,
        compiler_params=pltpu.CompilerParams(vmem_limit_bytes=28 << 20),
        cost_estimate=pl.CostEstimate(
            flops=6 * rows * depth * width, bytes_accessed=6 * depth * width, transcendentals=0
        ),
        name="project",
    )(owner, *args)


def attend_kernel(chip_ref, pair_ref, full_ref, start_ref, *refs):
    pieces, (out_ref, q_ref, k_ref, v_ref, top_ref, sum_ref, acc_ref) = refs[:-7], refs[-7:]
    chip = chip_ref[0]
    part = pieces[0].shape[2]
    rows = q_ref.shape[2]
    for chunk in range(rows // part):
        cols = slice(chunk * part, (chunk + 1) * part)
        for distance in range(4):
            piece = pieces[chunk * 4 + distance]
            for core in range(2):
                block = 2 * (chip ^ distance) + core
                q_ref[block, :, cols] = piece[core, :HD]
                k_ref[block, cols, :] = piece[core, HD : 2 * HD].T
                v_ref[block, :, cols] = piece[core, 2 * HD :]
    scale = HD ** (-0.5) * 1.4426950408889634

    def one_block(block, carry):
        token = block * rows + lax.broadcasted_iota(jnp.int32, (1, rows), 1)
        start = start_ref[block]
        top_ref[...] = jnp.full_like(top_ref, -1e30)
        sum_ref[...] = jnp.zeros_like(sum_ref)
        acc_ref[...] = jnp.zeros_like(acc_ref)

        def update(other, masked):
            scores = jnp.dot(k_ref[other], q_ref[block], preferred_element_type=jnp.float32) * scale
            if masked:
                key = other * rows + lax.broadcasted_iota(jnp.int32, (rows, rows), 0)
                scores = jnp.where((key >= start) & (key <= token), scores, -jnp.inf)
            newest = jnp.maximum(top_ref[...], jnp.max(scores, axis=0, keepdims=True))
            shrink = jnp.exp2(top_ref[...] - newest)
            weights = jnp.exp2(scores - newest)
            top_ref[...] = newest
            sum_ref[...] = sum_ref[...] * shrink + jnp.sum(weights, axis=0, keepdims=True)
            acc_ref[...] = acc_ref[...] * shrink + jnp.dot(
                v_ref[other], weights.astype(jnp.bfloat16), preferred_element_type=jnp.float32
            )

        def one_pair(other, inner):
            live = pair_ref[block, other] > 0
            whole = full_ref[block] <= other * rows

            @pl.when(live & whole & (other < block))
            def _():
                update(other, False)

            @pl.when(live & ~(whole & (other < block)))
            def _():
                update(other, True)

            return inner

        lax.fori_loop(0, block + 1, one_pair, 0)
        out_ref[block] = (acc_ref[...] / sum_ref[...]).astype(jnp.bfloat16)
        return carry

    lax.fori_loop(0, q_ref.shape[0], one_block, 0)


def attend(chip, pair_table, full, start, pieces):
    blocks, _, rows = start.shape
    smem = pl.BlockSpec(memory_space=pltpu.SMEM)
    vmem = pl.BlockSpec(memory_space=pltpu.VMEM)
    return pl.pallas_call(
        attend_kernel,
        in_specs=[smem, smem, smem, vmem] + [vmem] * len(pieces),
        out_specs=vmem,
        out_shape=jax.ShapeDtypeStruct((blocks, HD, rows), jnp.bfloat16),
        scratch_shapes=[
            pltpu.VMEM((blocks, HD, rows), jnp.bfloat16),
            pltpu.VMEM((blocks, rows, HD), jnp.bfloat16),
            pltpu.VMEM((blocks, HD, rows), jnp.bfloat16),
            pltpu.VMEM((1, rows), jnp.float32),
            pltpu.VMEM((1, rows), jnp.float32),
            pltpu.VMEM((HD, rows), jnp.float32),
        ],
        compiler_params=pltpu.CompilerParams(vmem_limit_bytes=28 << 20),
        cost_estimate=pl.CostEstimate(
            flops=25 * rows * rows * 4 * 128, bytes_accessed=8 << 20, transcendentals=25 * rows * rows
        ),
        name="attend",
    )(chip, pair_table, full, start, *pieces)


def swap(value, distance):
    count = lax.axis_size("blk")
    return lax.ppermute(value, "blk", [(place, place ^ distance) for place in range(count)])


def to_heads(sent):
    block = lax.axis_index("blk")
    chip, core = block // 2, block % 2
    by_core = sent.reshape((4, 2) + sent.shape[1:])
    kept = lax.dynamic_index_in_dim(by_core, core, 1, keepdims=False)
    given = lax.dynamic_index_in_dim(by_core, 1 - core, 1, keepdims=False)
    got = swap(given, 1)
    pieces = []
    for distance in range(4):
        from_kept = lax.dynamic_index_in_dim(kept, chip ^ distance, 0, keepdims=False)
        from_got = lax.dynamic_index_in_dim(got, chip ^ distance, 0, keepdims=False)
        pair = jnp.stack(
            [jnp.where(core == 0, from_kept, from_got), jnp.where(core == 0, from_got, from_kept)]
        )
        pieces.append(pair if distance == 0 else swap(pair, 2 * distance))
    return pieces


def to_blocks(mixed):
    block = lax.axis_index("blk")
    chip, core = block // 2, block % 2
    by_chip = mixed.reshape((4, 2) + mixed.shape[1:])
    held = []
    for distance in range(4):
        pair = lax.dynamic_index_in_dim(by_chip, chip ^ distance, 0, keepdims=False)
        held.append(pair if distance == 0 else swap(pair, 2 * distance))
    both = jnp.stack(held)
    kept = lax.dynamic_index_in_dim(both, core, 1, keepdims=False)
    got = swap(lax.dynamic_index_in_dim(both, 1 - core, 1, keepdims=False), 1)
    even = jnp.where(core == 0, kept, got)
    odd = jnp.where(core == 0, got, kept)
    heads = jnp.stack([even, odd], axis=1)
    heads = jnp.where(chip % 2 == 1, heads[jnp.array([1, 0, 3, 2])], heads)
    heads = jnp.where(chip // 2 == 1, heads[jnp.array([2, 3, 0, 1])], heads)
    return heads.reshape((8 * HD,) + mixed.shape[2:])


def combine_kernel(has_previous, is_last, index_ref, h_ref, w_ref, *refs):
    out_ref = refs[-1]
    weight = w_ref[...].reshape(h_ref.shape[0], out_ref.shape[1])
    product = lax.dot_general(
        h_ref[...], weight, (((0,), (0,)), ((), ())), preferred_element_type=jnp.float32
    )
    if has_previous:
        product = product + refs[0][...]
    out_ref[...] = product.astype(out_ref.dtype)


def combine(index, heads, weight, previous=None, is_last=False):
    depth, rows = heads.shape
    outer, _, inner, width = weight.shape
    tile = 512
    in_specs = [
        pl.BlockSpec((depth, rows), lambda s, o: (0, 0)),
        pl.BlockSpec((outer, 1, inner, tile), lambda s, o: (0, o[0], 0, s)),
    ]
    sums = pl.BlockSpec((rows, tile), lambda s, o: (0, s))
    args = [heads, weight]
    if previous is not None:
        in_specs.append(sums)
        args.append(previous)
    return pl.pallas_call(
        functools.partial(combine_kernel, previous is not None, is_last),
        grid_spec=pltpu.PrefetchScalarGridSpec(
            num_scalar_prefetch=1, grid=(width // tile,), in_specs=in_specs, out_specs=sums
        ),
        out_shape=jax.ShapeDtypeStruct((rows, width), jnp.bfloat16 if is_last else jnp.float32),
        compiler_params=pltpu.CompilerParams(vmem_limit_bytes=28 << 20),
        cost_estimate=pl.CostEstimate(
            flops=2 * rows * depth * width, bytes_accessed=2 * depth * width, transcendentals=0
        ),
        name="combine",
    )(index, *args)


def per_device_heads(hidden_in, ln_gain, w_qkv, w_out, doc_lengths, segment_ids, pair_table, page_table):
    rows, depth = hidden_in.shape
    part = rows // CHUNKS
    width = w_qkv.shape[2]
    block, place = lax.axis_index("blk"), lax.axis_index("tp")
    chip = block // 2
    blocks = lax.axis_size("blk")
    owners = [jnp.reshape(owner, (1,)).astype(jnp.int32) for owner in line_owners()]

    values32 = hidden_in.astype(jnp.float32)
    own_mean = jnp.mean(values32, axis=1)
    own_square = jnp.mean((values32 - own_mean[:, None]) ** 2, axis=1)
    stats = lax.all_gather(jnp.stack([own_mean, own_square]), "tp", axis=0)
    mean = jnp.mean(stats[:, 0], axis=0)
    variance = jnp.mean(stats[:, 1] + (stats[:, 0] - mean[None]) ** 2, axis=0)
    rstd = lax.rsqrt(variance + EPSILON)[:, None]
    mean = mean[:, None]
    gain = ln_gain.reshape(4, 1, depth)
    w3 = jnp.transpose(w_qkv, (1, 0, 2))

    token_index = block * rows + jnp.arange(rows, dtype=jnp.int32)
    positions = doc_positions(token_index, doc_lengths, segment_ids)
    frequency = 10000.0 ** (-(2.0 * jnp.arange(ROT // 2, dtype=jnp.float32)) / ROT)
    angles = positions.astype(jnp.float32)[None, :] * frequency[:, None]
    cosine, sine = jnp.cos(angles), jnp.sin(angles)
    cosine = jnp.concatenate([cosine, cosine])
    sine = jnp.concatenate([-sine, sine])

    share = lax.dynamic_slice_in_dim(w_out, block * HD, HD, 0)
    columns = []
    for distance in (1, 2, 3):
        piece = lax.dynamic_slice_in_dim(share, (place + distance) % 4 * depth, depth, 1)
        columns.append(
            lax.ppermute(piece, "tp", [(source, (source + distance) % 4) for source in range(4)])
        )
    others = lax.all_gather(jnp.stack(columns), "blk", axis=0)
    own = lax.dynamic_slice_in_dim(w_out, place * depth, depth, 1).reshape(1, 1, width, depth)

    sent, pieces = [], []
    for chunk in range(CHUNKS):
        cut = slice(chunk * part, (chunk + 1) * part)
        mine = hidden_in[cut]
        shards = [mine] + line_gather(mine)
        sums = None
        for step in range(4):
            tables = (cosine[:, cut], sine[:, cut]) if step == 3 else None
            sums = project(owners[step], shards[step], mean[cut], rstd[cut], gain, w3, sums, tables)
        sent.append(sums)
        pieces += to_heads(sums)

    ends = jnp.cumsum(doc_lengths)
    tokens = jnp.arange(blocks * rows, dtype=jnp.int32)
    start = jnp.max(jnp.where(ends[:, None] <= tokens[None, :], ends[:, None], 0), axis=0)
    start = start.astype(jnp.int32).reshape(blocks, 1, rows)
    mixed = attend(
        jnp.reshape(chip, (1,)).astype(jnp.int32), pair_table, start[:, 0, rows - 1], start, pieces
    )
    heads = to_blocks(mixed)

    results = []
    for chunk in range(CHUNKS):
        mine = heads[:, chunk * part : (chunk + 1) * part]
        shards = [mine] + line_gather(mine)
        sums = combine(jnp.zeros((1,), jnp.int32), shards[0], own)
        for step in range(1, 4):
            index = (place - owners[step]) % 4 - 1
            sums = combine(index, shards[step], others, sums, step == 3)
        results.append(sums)
    attn_out = jnp.concatenate(results, axis=0)

    page_count = rows // PAGE
    local_pages = page_table - block * page_count
    whole = jnp.concatenate(sent, axis=2)
    keys = whole[:, HD : 2 * HD].reshape(width, rows).T
    values = whole[:, 2 * HD :].reshape(width, rows).T
    stacked = jnp.stack([keys, values]).reshape(2, page_count, PAGE, width)
    page_cache = jnp.zeros_like(stacked).at[:, local_pages].set(stacked)
    return (attn_out, page_cache)


def solution(mesh):
    placed = (P("blk", "tp"), P(), P(None, None, "tp"), P("tp", None), P(), P("blk"), P(), P("blk"))

    def per_device(hidden_in, ln_gain, w_qkv, *rest):
        heads = w_qkv.shape[2] // HD
        fits = mesh.shape["tp"] == 4 and mesh.shape["blk"] == 8 and heads == 8
        form = per_device_heads if fits else per_device_any
        return form(hidden_in, ln_gain, w_qkv, *rest)

    return jax.shard_map(
        per_device,
        mesh=mesh,
        in_specs=placed,
        out_specs=(P("blk", "tp"), P(None, "blk", None, "tp")),
        check_vma=False,
    )
```

```python
import functools

import jax
import jax.numpy as jnp
from jax import lax
from jax.experimental import pallas as pl
from jax.experimental.pallas import tpu as pltpu
from jax.sharding import PartitionSpec as P

HD = 96
ROT = 24
PAGE = 16


EPSILON = 1e-05


def from_behind(value, axis, steps):
    count = lax.axis_size(axis)
    first, last = (max(0, -steps), min(count, count - steps))
    return lax.ppermute(value, axis, [(source, source + steps) for source in range(first, last)])


def layer_norm(whole, ln_gain):
    values32 = whole.astype(jnp.float32)
    row_mean = jnp.mean(values32, axis=-1, keepdims=True)
    centred = values32 - row_mean
    row_var = jnp.mean(centred * centred, axis=-1, keepdims=True)
    return (centred * lax.rsqrt(row_var + EPSILON) * ln_gain).astype(jnp.bfloat16)


def doc_positions(token_index, doc_lengths, segment_ids):
    starts = jnp.cumsum(doc_lengths) - doc_lengths
    slots = jnp.arange(doc_lengths.shape[0], dtype=jnp.int32)
    in_document = segment_ids[:, None] == slots[None, :]
    offsets = jnp.sum(jnp.where(in_document, starts[None, :], 0), axis=1)
    return token_index - offsets


def rotary(head_block, positions):
    half_rot = ROT // 2
    frequency = 10000.0 ** (-(2.0 * jnp.arange(half_rot, dtype=jnp.float32)) / ROT)
    angles = positions.astype(jnp.float32)[:, None] * frequency[None, :]
    cosine = jnp.cos(angles)[:, None, :]
    sine_part = jnp.sin(angles)[:, None, :]
    lower_half = head_block[..., :half_rot]
    upper_half = head_block[..., half_rot:ROT]
    return jnp.concatenate(
        [
            lower_half * cosine - upper_half * sine_part,
            upper_half * cosine + lower_half * sine_part,
            head_block[..., ROT:],
        ],
        axis=-1,
    )


def per_device_any(hidden_in, ln_gain, w_qkv, w_out, doc_lengths, segment_ids, pair_table, page_table):
    row_count = hidden_in.shape[0]
    whole = lax.all_gather(hidden_in, "tp", axis=1, tiled=True)
    normed = layer_norm(whole, ln_gain)
    col_count = w_qkv.shape[2]
    head_count = col_count // HD
    projected = jnp.einsum("tk,kcn->ctn", normed, w_qkv, preferred_element_type=jnp.float32)
    projected = projected.reshape(3, row_count, head_count, HD)
    block_index = lax.axis_index("blk")
    token_index = block_index * row_count + jnp.arange(row_count, dtype=jnp.int32)
    positions = doc_positions(token_index, doc_lengths, segment_ids)
    queries = rotary(projected[0], positions).astype(jnp.bfloat16)
    key_rows = rotary(projected[1], positions).astype(jnp.bfloat16)
    values = projected[2].astype(jnp.bfloat16)
    table_row = lax.dynamic_index_in_dim(pair_table, block_index, 0, keepdims=False)
    block_ids = jnp.arange(pair_table.shape[1], dtype=jnp.int32)
    scale = HD ** (-0.5)

    def attend(running, incoming, offset):
        key_piece, value_piece, segment_piece = incoming
        piece_rows = key_piece.shape[0]
        key_index = offset + jnp.arange(piece_rows, dtype=jnp.int32)
        matches = (key_index // row_count)[:, None] == block_ids[None, :]
        live = jnp.sum(jnp.where(matches, table_row[None, :], 0), axis=1) > 0

        def compute(previous):
            maxima, totals, weighted = previous
            scores = (
                jnp.einsum("qhd,khd->hqk", queries, key_piece, preferred_element_type=jnp.float32)
                * scale
            )
            allowed = (
                live[None, :]
                & (segment_ids[:, None] == segment_piece[None, :])
                & (key_index[None, :] <= token_index[:, None])
            )
            scores = jnp.where(allowed[None], scores, -jnp.inf)
            newest = jnp.maximum(maxima, jnp.max(scores, axis=-1))
            shrink = jnp.exp(maxima - newest)
            weights = jnp.exp(scores - newest[..., None])
            totals = totals * shrink + jnp.sum(weights, axis=-1)
            weighted = weighted * shrink[..., None] + jnp.einsum(
                "hqk,khd->hqd",
                weights.astype(jnp.bfloat16),
                value_piece,
                preferred_element_type=jnp.float32,
            )
            return (newest, totals, weighted)

        return lax.cond(jnp.any(live), compute, lambda previous: previous, running)

    start_state = (
        jnp.full((head_count, row_count), -1e30, jnp.float32),
        jnp.zeros((head_count, row_count), jnp.float32),
        jnp.zeros((head_count, row_count, HD), jnp.float32),
    )
    final = attend(start_state, (key_rows, values, segment_ids), block_index * row_count)
    for distance in range(1, lax.axis_size("blk") // 2 + 1):
        earlier = from_behind((key_rows, values, segment_ids), "blk", distance)
        final = attend(final, earlier, (block_index - distance) * row_count)
    mixed = (final[2] / final[1][..., None]).astype(jnp.bfloat16)
    heads_out = jnp.transpose(mixed, (1, 0, 2)).reshape(row_count, col_count)
    partial_term = jnp.dot(heads_out, w_out, preferred_element_type=jnp.float32)
    attn_out = lax.psum_scatter(
        partial_term.astype(jnp.bfloat16), "tp", scatter_dimension=1, tiled=True
    )
    page_count = row_count // PAGE
    local_pages = page_table - block_index * page_count
    stacked = jnp.stack(
        [key_rows.reshape(page_count, PAGE, col_count), values.reshape(page_count, PAGE, col_count)]
    )
    page_cache = jnp.zeros_like(stacked).at[:, local_pages].set(stacked)
    return (attn_out, page_cache)


def turn(value, distance):
    return lax.ppermute(value, "tp", [(source, (source + distance) % 4) for source in range(4)])


def line_hop(up, down, ups, downs):
    return lax.ppermute(up, "tp", ups), lax.ppermute(down, "tp", downs)


def line_owners():
    place = lax.axis_index("tp")
    first = jnp.where(place == 0, 1, place - 1)
    second = jnp.where(place == 0, 2, jnp.where(place == 3, 1, place + 1))
    third = jnp.where(place < 2, 3, 0)
    pick_second = jnp.where(place == 0, 1, jnp.where(place == 3, 2, 0))
    outer = (place == 0) | (place == 3)
    return [(place, 0 * place), (first, place == 0), (second, pick_second), (third, outer)]


def gather_line(value, work):
    up1, down1 = line_hop(value, value, [(0, 1), (1, 2), (2, 3)], [(3, 2), (2, 1), (1, 0)])
    work(0, [value])
    up2, down2 = line_hop(up1, down1, [(1, 2), (2, 3)], [(2, 1), (1, 0)])
    work(1, [up1, down1])
    inner = jnp.where(lax.axis_index("tp") == 2, up2, down2)
    outer = lax.ppermute(inner, "tp", [(2, 3), (1, 0)])
    work(2, [down1, down2, up2])
    work(3, [inner, outer])


OWNER, PICK, COLUMN, CHIP, CORE, LAST = 0, 4, 8, 12, 13, 14


def project_kernel(step, count, facts_ref, *refs):
    refs = list(refs)
    shards = refs[:count]
    mean_ref, rstd_ref, gain_ref, w_ref = refs[count : count + 4]
    del refs[: count + 4]
    previous_ref = refs.pop(0) if step > 0 else None
    kind = pl.program_id(0)
    normed_ref, turned_ref = refs[-2:]

    for pick, x_ref in enumerate(shards):

        @pl.when((kind == 0) & (facts_ref[PICK + step] == pick))
        def _():
            centred = x_ref[...].astype(jnp.float32) - mean_ref[...]
            normed_ref[...] = (centred * rstd_ref[...] * gain_ref[0]).astype(jnp.bfloat16)

    total = jnp.dot(normed_ref[...], w_ref[0], preferred_element_type=jnp.float32)
    if step > 0:
        total = total + previous_ref[0]
    if step < 3:
        refs[0][0] = total
        return
    cos_ref, sin_ref = refs[:2]
    kept_refs, given_ref = refs[2:6], refs[6]
    chip, core = facts_ref[CHIP], facts_ref[CORE]
    turned = total.T
    turned_ref[...] = turned.reshape(turned_ref.shape).astype(jnp.bfloat16)

    @pl.when(kind < 2)
    def _():
        half = ROT // 2
        for head in range(turned_ref.shape[0]):
            part = turned[head * HD : head * HD + ROT]
            swapped = jnp.concatenate([part[half:], part[:half]], axis=0)
            turned_ref[head, :ROT] = (part * cos_ref[...] + swapped * sin_ref[...]).astype(jnp.bfloat16)

    for distance in range(4):
        head = 2 * (chip ^ distance)
        kept_refs[distance][...] = turned_ref[head + core]
        given_ref[distance] = turned_ref[head + 1 - core]


def project(step, facts, shards, mean, rstd, gain, w3, previous, tables):
    rows, depth = shards[0].shape
    width = w3.shape[2]
    column = pl.BlockSpec((rows, 1), lambda c, o: (0, 0))
    in_specs = [pl.BlockSpec((rows, depth), lambda c, o: (0, 0)) for _ in shards] + [
        column,
        column,
        pl.BlockSpec((1, 1, depth), lambda c, o: (o[OWNER + step], 0, 0)),
        pl.BlockSpec((1, depth, width), lambda c, o: (c, o[OWNER + step], 0)),
    ]
    args = [*shards, mean, rstd, gain, w3]
    sums = pl.BlockSpec((1, rows, width), lambda c, o: (c, 0, 0))
    if step > 0:
        in_specs.append(sums)
        args.append(previous)
    out_shape, out_specs = jax.ShapeDtypeStruct((3, rows, width), jnp.float32), sums
    if step == 3:
        in_specs += [pl.BlockSpec((ROT, rows), lambda c, o: (0, 0))] * 2
        args += tables
        out_shape = [jax.ShapeDtypeStruct((3 * HD, rows), jnp.bfloat16)] * 4
        out_shape.append(jax.ShapeDtypeStruct((4, 3 * HD, rows), jnp.bfloat16))
        out_specs = [pl.BlockSpec((HD, rows), lambda c, o: (c, 0))] * 4
        out_specs.append(pl.BlockSpec((4, HD, rows), lambda c, o: (0, c, 0)))
    return pl.pallas_call(
        functools.partial(project_kernel, step, len(shards)),
        grid_spec=pltpu.PrefetchScalarGridSpec(
            num_scalar_prefetch=1,
            grid=(3,),
            in_specs=in_specs,
            out_specs=out_specs,
            scratch_shapes=[
                pltpu.VMEM((rows, depth), jnp.bfloat16),
                pltpu.VMEM((width // HD, HD, rows), jnp.bfloat16),
            ],
        ),
        out_shape=out_shape,
        compiler_params=pltpu.CompilerParams(vmem_limit_bytes=48 << 20),
        cost_estimate=pl.CostEstimate(
            flops=24 * rows * depth * width, bytes_accessed=6 * depth * width, transcendentals=0
        ),
        name="project",
    )(facts, *args)


def attend_kernel(facts_ref, pair_ref, start_ref, *refs):
    pieces, outs, (q_ref, k_ref, v_ref, top_ref, sum_ref, acc_ref) = refs[:-10], refs[-10:-6], refs[-6:]
    chip, own_core = facts_ref[CHIP], facts_ref[CORE]
    rows = q_ref.shape[2]
    for distance in range(4):
        for other, piece in enumerate(pieces[2 * distance : 2 * distance + 2]):
            block = 2 * (chip ^ distance) + (own_core ^ other)
            q_ref[block] = piece[:HD]
            k_ref[block] = piece[HD : 2 * HD].T
            v_ref[block] = piece[2 * HD :]
    scale = HD ** (-0.5) * 1.4426950408889634

    def one_block(block, carry):
        token = block * rows + lax.broadcasted_iota(jnp.int32, (1, rows), 1)
        start = start_ref[block]
        top_ref[...] = jnp.full_like(top_ref, -1e30)
        sum_ref[...] = jnp.zeros_like(sum_ref)
        acc_ref[...] = jnp.zeros_like(acc_ref)

        def update(other, masked):
            scores = jnp.dot(k_ref[other], q_ref[block], preferred_element_type=jnp.float32) * scale
            if masked:
                key = other * rows + lax.broadcasted_iota(jnp.int32, (rows, rows), 0)
                scores = jnp.where((key >= start) & (key <= token), scores, -jnp.inf)
            newest = jnp.maximum(top_ref[...], jnp.max(scores, axis=0, keepdims=True))
            shrink = jnp.exp2(top_ref[...] - newest)
            weights = jnp.exp2(scores - newest)
            top_ref[...] = newest
            sum_ref[...] = sum_ref[...] * shrink + jnp.sum(weights, axis=0, keepdims=True)
            acc_ref[...] = acc_ref[...] * shrink + jnp.dot(
                v_ref[other], weights.astype(jnp.bfloat16), preferred_element_type=jnp.float32
            )

        def one_pair(other, inner):
            live = pair_ref[block, other] > 0
            whole = facts_ref[LAST + block] <= other * rows

            @pl.when(live & whole & (other < block))
            def _():
                update(other, False)

            @pl.when(live & ~(whole & (other < block)))
            def _():
                update(other, True)

            return inner

        lax.fori_loop(0, block + 1, one_pair, 0)
        mixed = (acc_ref[...] / sum_ref[...]).astype(jnp.bfloat16)
        for distance, out_ref in enumerate(outs):

            @pl.when((block // 2) ^ chip == distance)
            def _():
                out_ref[block % 2] = mixed

        return carry

    lax.fori_loop(0, q_ref.shape[0], one_block, 0)


def attend(facts, pair_table, start, pieces):
    blocks, _, rows = start.shape
    smem = pl.BlockSpec(memory_space=pltpu.SMEM)
    vmem = pl.BlockSpec(memory_space=pltpu.VMEM)
    return pl.pallas_call(
        attend_kernel,
        in_specs=[smem, smem, vmem] + [vmem] * len(pieces),
        out_specs=[vmem] * 4,
        out_shape=[jax.ShapeDtypeStruct((2, HD, rows), jnp.bfloat16)] * 4,
        scratch_shapes=[
            pltpu.VMEM((blocks, HD, rows), jnp.bfloat16),
            pltpu.VMEM((blocks, rows, HD), jnp.bfloat16),
            pltpu.VMEM((blocks, HD, rows), jnp.bfloat16),
            pltpu.VMEM((1, rows), jnp.float32),
            pltpu.VMEM((1, rows), jnp.float32),
            pltpu.VMEM((HD, rows), jnp.float32),
        ],
        compiler_params=pltpu.CompilerParams(vmem_limit_bytes=28 << 20),
        cost_estimate=pl.CostEstimate(flops=1000, bytes_accessed=1000, transcendentals=0),
        name="attend",
    )(facts, pair_table, start, *pieces)


def swap(value, distance):
    count = lax.axis_size("blk")
    return lax.ppermute(value, "blk", [(place, place ^ distance) for place in range(count)])


def to_heads(kept, got):
    pieces = []
    for distance in range(4):
        for value in (kept[distance], got[distance]):
            pieces.append(value if distance == 0 else swap(value, 2 * distance))
    return pieces


def order_kernel(facts_ref, *refs):
    pairs, got_ref, out_ref = refs[:4], refs[4], refs[5]
    chip, core = facts_ref[CHIP], facts_ref[CORE]
    for distance in range(4):
        head = 2 * (chip ^ distance)
        out_ref[head + core] = pairs[distance][core]
        out_ref[head + 1 - core] = got_ref[distance]


def to_blocks(facts, mixed):
    core = lax.axis_index("blk") % 2
    held = [pair if distance == 0 else swap(pair, 2 * distance) for distance, pair in enumerate(mixed)]
    given = [lax.dynamic_index_in_dim(pair, 1 - core, 0, keepdims=False) for pair in held]
    got = swap(jnp.stack(given), 1)
    vmem = pl.BlockSpec(memory_space=pltpu.VMEM)
    heads = pl.pallas_call(
        order_kernel,
        in_specs=[pl.BlockSpec(memory_space=pltpu.SMEM)] + [vmem] * 5,
        out_specs=vmem,
        out_shape=jax.ShapeDtypeStruct((8,) + got.shape[1:], got.dtype),
        cost_estimate=pl.CostEstimate(flops=0, bytes_accessed=2 << 20, transcendentals=0),
        name="order",
    )(facts, *held, got)
    return heads.reshape((8 * HD,) + got.shape[2:])


def combine_kernel(steps, counts, facts_ref, *refs):
    refs = list(refs)
    arrays = []
    for count in counts:
        arrays.append(refs[:count])
        del refs[:count]
    own_ref, others_ref = (refs.pop(0) if 0 in steps else None), refs.pop(0)
    previous_ref = refs.pop(0) if 0 not in steps else None
    out_ref, sum_ref = refs
    slot = pl.program_id(1)
    for place, step in enumerate(steps):
        for pick, h_ref in enumerate(arrays[place]):

            @pl.when((slot == place) & (facts_ref[PICK + step] == pick))
            def _():
                w_ref = own_ref if step == 0 else others_ref
                product = lax.dot_general(
                    h_ref[...],
                    w_ref[...].reshape(h_ref.shape[0], out_ref.shape[1]),
                    (((0,), (0,)), ((), ())),
                    preferred_element_type=jnp.float32,
                )
                if place > 0:
                    product = product + sum_ref[...]
                elif previous_ref is not None:
                    product = product + previous_ref[...].astype(jnp.float32)
                if place < len(steps) - 1:
                    sum_ref[...] = product
                else:
                    out_ref[...] = product.astype(out_ref.dtype)


def combine(steps, facts, arrays, own, others, previous=None):
    depth, rows = arrays[-1][-1].shape
    outer, _, inner, width = others.shape
    tile = width // 2
    out_spec = pl.BlockSpec((rows, tile), lambda n, k, o: (0, n))
    in_specs = [pl.BlockSpec((depth, rows), lambda n, k, o: (0, 0)) for step in arrays for _ in step]
    args = [array for step in arrays for array in step]
    if 0 in steps:
        in_specs.append(pl.BlockSpec((1, 1, depth, tile), lambda n, k, o: (0, 0, 0, n)))
        args.append(own)
    in_specs.append(
        pl.BlockSpec((outer, 1, inner, tile), lambda n, k, o: (0, o[COLUMN + steps[0] + k], 0, n))
    )
    args.append(others)
    if 0 not in steps:
        in_specs.append(out_spec)
        args.append(previous)
    return pl.pallas_call(
        functools.partial(combine_kernel, steps, tuple(len(step) for step in arrays)),
        grid_spec=pltpu.PrefetchScalarGridSpec(
            num_scalar_prefetch=1,
            grid=(width // tile, len(steps)),
            in_specs=in_specs,
            out_specs=out_spec,
            scratch_shapes=[pltpu.VMEM((rows, tile), jnp.float32)],
        ),
        out_shape=jax.ShapeDtypeStruct((rows, width), jnp.bfloat16),
        compiler_params=pltpu.CompilerParams(vmem_limit_bytes=56 << 20),
        cost_estimate=pl.CostEstimate(
            flops=4 * len(steps) * rows * depth * width,
            bytes_accessed=2 * len(steps) * depth * width,
            transcendentals=0,
        ),
        name="combine",
    )(facts, *args)


def share_kernel(facts_ref, w_ref, *refs):
    outs, sems = refs[-4:-1], refs[-1]
    rows, width = outs[0].shape
    first = facts_ref[0] * rows
    copies = []
    for place, out_ref in enumerate(outs):
        begin = pl.multiple_of(facts_ref[1 + place] * width, width)
        window = w_ref.at[pl.ds(pl.multiple_of(first, rows), rows), pl.ds(begin, width)]
        copies.append(pltpu.make_async_copy(window, out_ref, sems.at[place]))
    for copy in copies:
        copy.start()
    for copy in copies:
        copy.wait()


def shares(numbers, w_out, width, waited):
    any_space = pl.BlockSpec(memory_space=pl.ANY)
    return pl.pallas_call(
        share_kernel,
        in_specs=[pl.BlockSpec(memory_space=pltpu.SMEM), any_space] + [any_space] * len(waited),
        out_specs=[pl.BlockSpec(memory_space=pltpu.VMEM)] * 3,
        out_shape=[jax.ShapeDtypeStruct((HD, width), w_out.dtype)] * 3,
        scratch_shapes=[pltpu.SemaphoreType.DMA((3,))],
        cost_estimate=pl.CostEstimate(flops=0, bytes_accessed=2 << 20, transcendentals=0),
        name="shares",
    )(numbers, w_out, *waited)


def stack_kernel(*refs):
    for place in range(3):
        refs[-1][place] = refs[place][...]


def stack(values, waited):
    any_space, vmem = pl.BlockSpec(memory_space=pl.ANY), pl.BlockSpec(memory_space=pltpu.VMEM)
    return pl.pallas_call(
        stack_kernel,
        in_specs=[vmem] * 3 + [any_space] * len(waited),
        out_specs=vmem,
        out_shape=jax.ShapeDtypeStruct((3,) + values[0].shape, values[0].dtype),
        cost_estimate=pl.CostEstimate(flops=0, bytes_accessed=2 << 20, transcendentals=0),
        name="stack",
    )(*values, *waited)


def pages_kernel(facts_ref, *refs):
    kept_refs, given_ref, out_ref, turned_ref = refs[:4], refs[4], refs[5], refs[6]
    blocks = facts_ref.shape[0] - LAST - out_ref.shape[1]
    chip, core = facts_ref[CHIP], facts_ref[CORE]
    for tile in range(given_ref.shape[2] // 128):
        tokens = slice(tile * 128, (tile + 1) * 128)
        for kind in range(2):
            entries = slice((kind + 1) * HD, (kind + 2) * HD)
            for distance in range(4):
                head = 2 * (chip ^ distance)
                turned_ref[head + core] = kept_refs[distance][entries, tokens]
                turned_ref[head + 1 - core] = given_ref[distance, entries, tokens]
            turned = turned_ref[...].reshape(8 * HD, 128).T
            for page in range(128 // PAGE):
                place = facts_ref[LAST + blocks + tile * 128 // PAGE + page]
                out_ref[kind, place] = turned[page * PAGE : (page + 1) * PAGE]


def pages(facts, count, parts):
    width = 8 * HD
    vmem = pl.BlockSpec(memory_space=pltpu.VMEM)
    return pl.pallas_call(
        pages_kernel,
        in_specs=[pl.BlockSpec(memory_space=pltpu.SMEM)] + [vmem] * len(parts),
        out_specs=vmem,
        scratch_shapes=[pltpu.VMEM((8, HD, 128), jnp.bfloat16)],
        out_shape=jax.ShapeDtypeStruct((2, count, PAGE, width), jnp.bfloat16),
        compiler_params=pltpu.CompilerParams(vmem_limit_bytes=56 << 20),
        cost_estimate=pl.CostEstimate(flops=0, bytes_accessed=10 << 20, transcendentals=0),
        name="pages",
    )(facts, *parts)


def per_device_heads(hidden_in, ln_gain, w_qkv, w_out, doc_lengths, segment_ids, pair_table, page_table):
    rows, depth = hidden_in.shape
    width = w_qkv.shape[2]
    block, place = lax.axis_index("blk"), lax.axis_index("tp")
    chip = block // 2
    blocks = lax.axis_size("blk")
    values32 = hidden_in.astype(jnp.float32)
    own_mean = jnp.mean(values32, axis=1)
    own_square = jnp.mean((values32 - own_mean[:, None]) ** 2, axis=1)
    own_stats = jnp.stack([own_mean, own_square])
    stats = jnp.stack([own_stats] + [turn(own_stats, distance) for distance in (1, 2, 3)])
    mean = jnp.mean(stats[:, 0], axis=0)
    variance = jnp.mean(stats[:, 1] + (stats[:, 0] - mean[None]) ** 2, axis=0)
    rstd = lax.rsqrt(variance + EPSILON)[:, None]
    mean = mean[:, None]
    gain = ln_gain.reshape(4, 1, depth)
    w3 = jnp.transpose(w_qkv, (1, 0, 2))

    token_index = block * rows + jnp.arange(rows, dtype=jnp.int32)
    positions = doc_positions(token_index, doc_lengths, segment_ids)
    frequency = 10000.0 ** (-(2.0 * jnp.arange(ROT // 2, dtype=jnp.float32)) / ROT)
    angles = positions.astype(jnp.float32)[None, :] * frequency[:, None]
    cosine, sine = jnp.cos(angles), jnp.sin(angles)
    cosine = jnp.concatenate([cosine, cosine])
    sine = jnp.concatenate([-sine, sine])

    ends = jnp.cumsum(doc_lengths)
    tokens = jnp.arange(blocks * rows, dtype=jnp.int32)
    start = jnp.max(jnp.where(ends[:, None] <= tokens[None, :], ends[:, None], 0), axis=0)
    start = start.astype(jnp.int32).reshape(blocks, 1, rows)
    page_count = rows // PAGE
    steps = line_owners()
    numbers = [owner for owner, _ in steps] + [pick for _, pick in steps]
    numbers += [jnp.maximum((place - owner) % 4 - 1, 0) for owner, _ in steps] + [chip, block % 2]
    facts = jnp.concatenate(
        [
            jnp.stack([jnp.asarray(number).astype(jnp.int32) for number in numbers]),
            start[:, 0, rows - 1],
            page_table - block * page_count,
        ]
    )

    total = [None]

    def take_in(step, arrays):
        total[0] = project(
            step, facts, arrays, mean, rstd, gain, w3, total[0], [cosine, sine]
        )

    gather_line(hidden_in, take_in)
    *kept, given = total[0]
    arrived = to_heads(kept, swap(given, 1))
    page_cache = pages(facts, page_count, [*kept, given])

    windows = jnp.stack([block] + [(place + distance) % 4 for distance in (1, 2, 3)]).astype(jnp.int32)
    windows = shares(windows, w_out, depth, [arrived[5], arrived[7]])
    columns = [turn(window, distance) for distance, window in zip((1, 2, 3), windows)]
    mixed = attend(facts, pair_table, start, arrived)
    others = lax.all_gather(stack(columns, mixed[:1]), "blk", axis=0)
    heads = to_blocks(facts, mixed)
    own = lax.dynamic_slice_in_dim(w_out, place * depth, depth, 1).reshape(1, 1, width, depth)

    came, result = [], [None]

    def add_in(step, arrays):
        came.append(arrays)
        if step == 2:
            result[0] = combine((0, 1, 2), facts, came[:3], own, others)
        if step == 3:
            result[0] = combine((3,), facts, came[3:], own, others, result[0])

    gather_line(heads, add_in)
    attn_out = result[0]
    return (attn_out, page_cache)


def solution(mesh):
    placed = (P("blk", "tp"), P(), P(None, None, "tp"), P("tp", None), P(), P("blk"), P(), P("blk"))

    def per_device(hidden_in, ln_gain, w_qkv, *rest):
        heads = w_qkv.shape[2] // HD
        fits = mesh.shape["tp"] == 4 and mesh.shape["blk"] == 8 and heads == 8
        form = per_device_heads if fits else per_device_any
        return form(hidden_in, ln_gain, w_qkv, *rest)

    return jax.shard_map(
        per_device,
        mesh=mesh,
        in_specs=placed,
        out_specs=(P("blk", "tp"), P(None, "blk", None, "tp")),
        check_vma=False,
    )
```

```python
import functools

import jax
import jax.numpy as jnp
from jax import lax
from jax.experimental import pallas as pl
from jax.experimental.pallas import tpu as pltpu
from jax.sharding import PartitionSpec as P

HD = 96
ROT = 24
PAGE = 16


EPSILON = 1e-05
QUERY_SCALE = HD ** (-0.5) * 1.4426950408889634


def from_behind(value, axis, steps):
    count = lax.axis_size(axis)
    first, last = (max(0, -steps), min(count, count - steps))
    return lax.ppermute(value, axis, [(source, source + steps) for source in range(first, last)])


def layer_norm(whole, ln_gain):
    values32 = whole.astype(jnp.float32)
    row_mean = jnp.mean(values32, axis=-1, keepdims=True)
    centred = values32 - row_mean
    row_var = jnp.mean(centred * centred, axis=-1, keepdims=True)
    return (centred * lax.rsqrt(row_var + EPSILON) * ln_gain).astype(jnp.bfloat16)


def doc_positions(token_index, doc_lengths, segment_ids):
    starts = jnp.cumsum(doc_lengths) - doc_lengths
    slots = jnp.arange(doc_lengths.shape[0], dtype=jnp.int32)
    in_document = segment_ids[:, None] == slots[None, :]
    offsets = jnp.sum(jnp.where(in_document, starts[None, :], 0), axis=1)
    return token_index - offsets


def rotary(head_block, positions):
    half_rot = ROT // 2
    frequency = 10000.0 ** (-(2.0 * jnp.arange(half_rot, dtype=jnp.float32)) / ROT)
    angles = positions.astype(jnp.float32)[:, None] * frequency[None, :]
    cosine = jnp.cos(angles)[:, None, :]
    sine_part = jnp.sin(angles)[:, None, :]
    lower_half = head_block[..., :half_rot]
    upper_half = head_block[..., half_rot:ROT]
    return jnp.concatenate(
        [
            lower_half * cosine - upper_half * sine_part,
            upper_half * cosine + lower_half * sine_part,
            head_block[..., ROT:],
        ],
        axis=-1,
    )


def per_device_any(hidden_in, ln_gain, w_qkv, w_out, doc_lengths, segment_ids, pair_table, page_table):
    row_count = hidden_in.shape[0]
    whole = lax.all_gather(hidden_in, "tp", axis=1, tiled=True)
    normed = layer_norm(whole, ln_gain)
    col_count = w_qkv.shape[2]
    head_count = col_count // HD
    projected = jnp.einsum("tk,kcn->ctn", normed, w_qkv, preferred_element_type=jnp.float32)
    projected = projected.reshape(3, row_count, head_count, HD)
    block_index = lax.axis_index("blk")
    token_index = block_index * row_count + jnp.arange(row_count, dtype=jnp.int32)
    positions = doc_positions(token_index, doc_lengths, segment_ids)
    queries = rotary(projected[0], positions).astype(jnp.bfloat16)
    key_rows = rotary(projected[1], positions).astype(jnp.bfloat16)
    values = projected[2].astype(jnp.bfloat16)
    table_row = lax.dynamic_index_in_dim(pair_table, block_index, 0, keepdims=False)
    block_ids = jnp.arange(pair_table.shape[1], dtype=jnp.int32)
    scale = HD ** (-0.5)

    def attend(running, incoming, offset):
        key_piece, value_piece, segment_piece = incoming
        piece_rows = key_piece.shape[0]
        key_index = offset + jnp.arange(piece_rows, dtype=jnp.int32)
        matches = (key_index // row_count)[:, None] == block_ids[None, :]
        live = jnp.sum(jnp.where(matches, table_row[None, :], 0), axis=1) > 0

        def compute(previous):
            maxima, totals, weighted = previous
            scores = (
                jnp.einsum("qhd,khd->hqk", queries, key_piece, preferred_element_type=jnp.float32)
                * scale
            )
            allowed = (
                live[None, :]
                & (segment_ids[:, None] == segment_piece[None, :])
                & (key_index[None, :] <= token_index[:, None])
            )
            scores = jnp.where(allowed[None], scores, -jnp.inf)
            newest = jnp.maximum(maxima, jnp.max(scores, axis=-1))
            shrink = jnp.exp(maxima - newest)
            weights = jnp.exp(scores - newest[..., None])
            totals = totals * shrink + jnp.sum(weights, axis=-1)
            weighted = weighted * shrink[..., None] + jnp.einsum(
                "hqk,khd->hqd",
                weights.astype(jnp.bfloat16),
                value_piece,
                preferred_element_type=jnp.float32,
            )
            return (newest, totals, weighted)

        return lax.cond(jnp.any(live), compute, lambda previous: previous, running)

    start_state = (
        jnp.full((head_count, row_count), -1e30, jnp.float32),
        jnp.zeros((head_count, row_count), jnp.float32),
        jnp.zeros((head_count, row_count, HD), jnp.float32),
    )
    final = attend(start_state, (key_rows, values, segment_ids), block_index * row_count)
    for distance in range(1, lax.axis_size("blk") // 2 + 1):
        earlier = from_behind((key_rows, values, segment_ids), "blk", distance)
        final = attend(final, earlier, (block_index - distance) * row_count)
    mixed = (final[2] / final[1][..., None]).astype(jnp.bfloat16)
    heads_out = jnp.transpose(mixed, (1, 0, 2)).reshape(row_count, col_count)
    partial_term = jnp.dot(heads_out, w_out, preferred_element_type=jnp.float32)
    attn_out = lax.psum_scatter(
        partial_term.astype(jnp.bfloat16), "tp", scatter_dimension=1, tiled=True
    )
    page_count = row_count // PAGE
    local_pages = page_table - block_index * page_count
    stacked = jnp.stack(
        [key_rows.reshape(page_count, PAGE, col_count), values.reshape(page_count, PAGE, col_count)]
    )
    page_cache = jnp.zeros_like(stacked).at[:, local_pages].set(stacked)
    return (attn_out, page_cache)


def turn(value, distance):
    return lax.ppermute(value, "tp", [(source, (source + distance) % 4) for source in range(4)])


def line_hop(up, down, ups, downs):
    return lax.ppermute(up, "tp", ups), lax.ppermute(down, "tp", downs)


def line_owners():
    place = lax.axis_index("tp")
    first = jnp.where(place == 0, 1, place - 1)
    second = jnp.where(place == 0, 2, jnp.where(place == 3, 1, place + 1))
    third = jnp.where(place < 2, 3, 0)
    pick_second = jnp.where(place == 0, 1, jnp.where(place == 3, 2, 0))
    outer = (place == 0) | (place == 3)
    return [(place, 0 * place), (first, place == 0), (second, pick_second), (third, outer)]


def gather_line(value, work):
    up1, down1 = line_hop(value, value, [(0, 1), (1, 2), (2, 3)], [(3, 2), (2, 1), (1, 0)])
    work(0, [value])
    up2, down2 = line_hop(up1, down1, [(1, 2), (2, 3)], [(2, 1), (1, 0)])
    work(1, [up1, down1])
    inner = jnp.where(lax.axis_index("tp") == 2, up2, down2)
    outer = lax.ppermute(inner, "tp", [(2, 3), (1, 0)])
    work(2, [down1, down2, up2])
    work(3, [inner, outer])


OWNER, PICK, COLUMN, CHIP, CORE, LAST = 0, 4, 8, 12, 13, 14


def project_kernel(step, count, facts_ref, *refs):
    refs = list(refs)
    shards = refs[:count]
    mean_ref, rstd_ref, gain_ref, w_ref = refs[count : count + 4]
    del refs[: count + 4]
    previous_ref = refs.pop(0) if step > 0 else None
    kind = pl.program_id(0)
    normed_ref, turned_ref = refs[-2:]

    for pick, x_ref in enumerate(shards):

        @pl.when((kind == 0) & (facts_ref[PICK + step] == pick))
        def _():
            centred = x_ref[...].astype(jnp.float32) - mean_ref[...]
            normed_ref[...] = (centred * rstd_ref[...] * gain_ref[0]).astype(jnp.bfloat16)

    total = jnp.dot(normed_ref[...], w_ref[0], preferred_element_type=jnp.float32)
    if step > 0:
        total = total + previous_ref[0]
    if step < 3:
        refs[0][0] = total
        return
    cos_ref, sin_ref = refs[:2]
    kept_refs, given_ref = refs[5:9], refs[9]
    chip, core = facts_ref[CHIP], facts_ref[CORE]
    turned = total.T * jnp.where(kind == 0, QUERY_SCALE, 1.0)
    turned_ref[...] = turned.reshape(turned_ref.shape).astype(jnp.bfloat16)

    @pl.when(kind < 2)
    def _():
        half = ROT // 2
        for head in range(turned_ref.shape[0]):
            part = turned[head * HD : head * HD + ROT]
            swapped = jnp.concatenate([part[half:], part[:half]], axis=0)
            turned_ref[head, :ROT] = (part * cos_ref[...] + swapped * sin_ref[...]).astype(jnp.bfloat16)

    for distance in range(4):
        head = 2 * (chip ^ distance)
        kept_refs[distance][...] = turned_ref[head + core]
        given_ref[distance] = turned_ref[head + 1 - core]


def project(step, facts, shards, mean, rstd, gain, w3, previous, tables, waited):
    rows, depth = shards[0].shape
    width = w3.shape[2]
    column = pl.BlockSpec((rows, 1), lambda c, o: (0, 0))
    in_specs = [pl.BlockSpec((rows, depth), lambda c, o: (0, 0)) for _ in shards] + [
        column,
        column,
        pl.BlockSpec((1, 1, depth), lambda c, o: (o[OWNER + step], 0, 0)),
        pl.BlockSpec((1, depth, width), lambda c, o: (c, o[OWNER + step], 0)),
    ]
    args = [*shards, mean, rstd, gain, w3]
    sums = pl.BlockSpec((1, rows, width), lambda c, o: (c, 0, 0))
    if step > 0:
        in_specs.append(sums)
        args.append(previous)
    out_shape, out_specs = jax.ShapeDtypeStruct((3, rows, width), jnp.float32), sums
    if step == 3:
        in_specs += [pl.BlockSpec((ROT, rows), lambda c, o: (0, 0))] * 2
        in_specs += [pl.BlockSpec(memory_space=pl.ANY)] * len(waited)
        args += tables + waited
        out_shape = [jax.ShapeDtypeStruct((3 * HD, rows), jnp.bfloat16)] * 4
        out_shape.append(jax.ShapeDtypeStruct((4, 3 * HD, rows), jnp.bfloat16))
        out_specs = [pl.BlockSpec((HD, rows), lambda c, o: (c, 0))] * 4
        out_specs.append(pl.BlockSpec((4, HD, rows), lambda c, o: (0, c, 0)))
    return pl.pallas_call(
        functools.partial(project_kernel, step, len(shards)),
        grid_spec=pltpu.PrefetchScalarGridSpec(
            num_scalar_prefetch=1,
            grid=(3,),
            in_specs=in_specs,
            out_specs=out_specs,
            scratch_shapes=[
                pltpu.VMEM((rows, depth), jnp.bfloat16),
                pltpu.VMEM((width // HD, HD, rows), jnp.bfloat16),
            ],
        ),
        out_shape=out_shape,
        compiler_params=pltpu.CompilerParams(vmem_limit_bytes=48 << 20),
        cost_estimate=pl.CostEstimate(
            flops=(1, 20, 20, 6)[step] * rows * depth * width, bytes_accessed=0, transcendentals=0
        ),
        name="project",
    )(facts, *args)


def attend_kernel(facts_ref, pair_ref, start_ref, *refs):
    pieces, outs, (q_ref, k_ref, v_ref, top_ref, sum_ref, acc_ref) = refs[:-10], refs[-10:-6], refs[-6:]
    chip, own_core = facts_ref[CHIP], facts_ref[CORE]
    rows = q_ref.shape[2]
    for distance in range(4):
        for other, piece in enumerate(pieces[2 * distance : 2 * distance + 2]):
            block = 2 * (chip ^ distance) + (own_core ^ other)
            q_ref[block] = piece[:HD]
            k_ref[block] = piece[HD : 2 * HD].T
            v_ref[block] = piece[2 * HD :]
    def one_block(block, carry):
        token = block * rows + lax.broadcasted_iota(jnp.int32, (1, rows), 1)
        start = start_ref[block]
        top_ref[...] = jnp.full_like(top_ref, -1e30)
        sum_ref[...] = jnp.zeros_like(sum_ref)
        acc_ref[...] = jnp.zeros_like(acc_ref)

        def update(other, masked):
            scores = jnp.dot(k_ref[other], q_ref[block], preferred_element_type=jnp.float32)
            if masked:
                key = other * rows + lax.broadcasted_iota(jnp.int32, (rows, rows), 0)
                scores = jnp.where((key >= start) & (key <= token), scores, -jnp.inf)
            newest = jnp.maximum(top_ref[...], jnp.max(scores, axis=0, keepdims=True))
            shrink = jnp.exp2(top_ref[...] - newest)
            weights = jnp.exp2(scores - newest)
            top_ref[...] = newest
            sum_ref[...] = sum_ref[...] * shrink + jnp.sum(weights, axis=0, keepdims=True)
            acc_ref[...] = acc_ref[...] * shrink + jnp.dot(
                v_ref[other], weights.astype(jnp.bfloat16), preferred_element_type=jnp.float32
            )

        def one_pair(other, inner):
            live = pair_ref[block, other] > 0
            whole = facts_ref[LAST + block] <= other * rows

            @pl.when(live & whole & (other < block))
            def _():
                update(other, False)

            @pl.when(live & ~(whole & (other < block)))
            def _():
                update(other, True)

            return inner

        lax.fori_loop(0, block + 1, one_pair, 0)
        mixed = (acc_ref[...] / sum_ref[...]).astype(jnp.bfloat16)
        for distance, out_ref in enumerate(outs):

            @pl.when((block // 2) ^ chip == distance)
            def _():
                out_ref[block % 2] = mixed

        return carry

    lax.fori_loop(0, q_ref.shape[0], one_block, 0)


def attend(facts, pair_table, start, pieces):
    blocks, _, rows = start.shape
    smem = pl.BlockSpec(memory_space=pltpu.SMEM)
    vmem = pl.BlockSpec(memory_space=pltpu.VMEM)
    return pl.pallas_call(
        attend_kernel,
        in_specs=[smem, smem, vmem] + [vmem] * len(pieces),
        out_specs=[vmem] * 4,
        out_shape=[jax.ShapeDtypeStruct((2, HD, rows), jnp.bfloat16)] * 4,
        scratch_shapes=[
            pltpu.VMEM((blocks, HD, rows), jnp.bfloat16),
            pltpu.VMEM((blocks, rows, HD), jnp.bfloat16),
            pltpu.VMEM((blocks, HD, rows), jnp.bfloat16),
            pltpu.VMEM((1, rows), jnp.float32),
            pltpu.VMEM((1, rows), jnp.float32),
            pltpu.VMEM((HD, rows), jnp.float32),
        ],
        compiler_params=pltpu.CompilerParams(vmem_limit_bytes=28 << 20),
        cost_estimate=pl.CostEstimate(flops=1000, bytes_accessed=1000, transcendentals=0),
        name="attend",
    )(facts, pair_table, start, *pieces)


def swap(value, distance):
    count = lax.axis_size("blk")
    return lax.ppermute(value, "blk", [(place, place ^ distance) for place in range(count)])


def to_heads(kept, got):
    pieces = []
    for distance in range(4):
        for value in (kept[distance], got[distance]):
            pieces.append(value if distance == 0 else swap(value, 2 * distance))
    return pieces


def order_kernel(facts_ref, *refs):
    pairs, got_ref, out_ref = refs[:4], refs[4], refs[5]
    chip, core = facts_ref[CHIP], facts_ref[CORE]
    for distance in range(4):
        head = 2 * (chip ^ distance)
        out_ref[head + core] = pairs[distance][core]
        out_ref[head + 1 - core] = got_ref[distance]


def to_blocks(facts, mixed):
    core = lax.axis_index("blk") % 2
    held = mixed[:1] + [swap(mixed[distance], 2 * distance) for distance in (1, 2, 3)]
    given = [lax.dynamic_index_in_dim(pair, 1 - core, 0, keepdims=False) for pair in held]
    got = swap(jnp.stack(given), 1)
    vmem = pl.BlockSpec(memory_space=pltpu.VMEM)
    heads = pl.pallas_call(
        order_kernel,
        in_specs=[pl.BlockSpec(memory_space=pltpu.SMEM)] + [vmem] * 5,
        out_specs=vmem,
        out_shape=jax.ShapeDtypeStruct((8,) + got.shape[1:], got.dtype),
        cost_estimate=pl.CostEstimate(flops=0, bytes_accessed=2 << 20, transcendentals=0),
        name="order",
    )(facts, *held, got)
    return heads.reshape((8 * HD,) + got.shape[2:])


def combine_kernel(steps, counts, facts_ref, *refs):
    refs = list(refs)
    arrays = []
    for count in counts:
        arrays.append(refs[:count])
        del refs[:count]
    own_ref, others_ref = (refs.pop(0) if 0 in steps else None), refs.pop(0)
    previous_ref = refs.pop(0) if 0 not in steps else None
    out_ref, sum_ref = refs
    slot = pl.program_id(1)
    for place, step in enumerate(steps):
        for pick, h_ref in enumerate(arrays[place]):

            @pl.when((slot == place) & (facts_ref[PICK + step] == pick))
            def _():
                w_ref = own_ref if step == 0 else others_ref
                product = lax.dot_general(
                    h_ref[...],
                    w_ref[...].reshape(h_ref.shape[0], out_ref.shape[1]),
                    (((0,), (0,)), ((), ())),
                    preferred_element_type=jnp.float32,
                )
                if place > 0:
                    product = product + sum_ref[...]
                elif previous_ref is not None:
                    product = product + previous_ref[...].astype(jnp.float32)
                if place < len(steps) - 1:
                    sum_ref[...] = product
                else:
                    out_ref[...] = product.astype(out_ref.dtype)


def combine(steps, facts, arrays, own, others, previous=None):
    depth, rows = arrays[-1][-1].shape
    outer, _, inner, width = others.shape
    tile = width // 2
    out_spec = pl.BlockSpec((rows, tile), lambda n, k, o: (0, n))
    in_specs = [pl.BlockSpec((depth, rows), lambda n, k, o: (0, 0)) for step in arrays for _ in step]
    args = [array for step in arrays for array in step]
    if 0 in steps:
        in_specs.append(
            pl.BlockSpec((depth, tile), lambda n, k, o: (0, o[OWNER] * (width // tile) + n))
        )
        args.append(own)
    in_specs.append(
        pl.BlockSpec((outer, 1, inner, tile), lambda n, k, o: (0, o[COLUMN + steps[0] + k], 0, n))
    )
    args.append(others)
    if 0 not in steps:
        in_specs.append(out_spec)
        args.append(previous)
    return pl.pallas_call(
        functools.partial(combine_kernel, steps, tuple(len(step) for step in arrays)),
        grid_spec=pltpu.PrefetchScalarGridSpec(
            num_scalar_prefetch=1,
            grid=(width // tile, len(steps)),
            in_specs=in_specs,
            out_specs=out_spec,
            scratch_shapes=[pltpu.VMEM((rows, tile), jnp.float32)],
        ),
        out_shape=jax.ShapeDtypeStruct((rows, width), jnp.bfloat16),
        compiler_params=pltpu.CompilerParams(vmem_limit_bytes=56 << 20),
        cost_estimate=pl.CostEstimate(
            flops=4 * len(steps) * rows * depth * width,
            bytes_accessed=2 * len(steps) * depth * width,
            transcendentals=0,
        ),
        name="combine",
    )(facts, *args)


def share_kernel(facts_ref, w_ref, *refs):
    outs, sems = refs[:3], refs[3]
    rows, width = outs[0].shape
    first = facts_ref[0] * rows
    copies = []
    for place, out_ref in enumerate(outs):
        begin = pl.multiple_of(facts_ref[1 + place] * width, width)
        window = w_ref.at[pl.ds(pl.multiple_of(first, rows), rows), pl.ds(begin, width)]
        copies.append(pltpu.make_async_copy(window, out_ref, sems.at[place]))
    for copy in copies:
        copy.start()
    for copy in copies:
        copy.wait()


def shares(numbers, w_out, width):
    any_space = pl.BlockSpec(memory_space=pl.ANY)
    return pl.pallas_call(
        share_kernel,
        in_specs=[pl.BlockSpec(memory_space=pltpu.SMEM), any_space],
        out_specs=[pl.BlockSpec(memory_space=pltpu.VMEM)] * 3,
        out_shape=[jax.ShapeDtypeStruct((HD, width), w_out.dtype)] * 3,
        scratch_shapes=[pltpu.SemaphoreType.DMA((3,))],
        cost_estimate=pl.CostEstimate(flops=0, bytes_accessed=2 << 20, transcendentals=0),
        name="shares",
    )(numbers, w_out)


def stack_kernel(*refs):
    for place in range(3):
        refs[-1][place] = refs[place][...]


def stack(values, waited):
    any_space, vmem = pl.BlockSpec(memory_space=pl.ANY), pl.BlockSpec(memory_space=pltpu.VMEM)
    return pl.pallas_call(
        stack_kernel,
        in_specs=[vmem] * 3 + [any_space] * len(waited),
        out_specs=vmem,
        out_shape=jax.ShapeDtypeStruct((3,) + values[0].shape, values[0].dtype),
        cost_estimate=pl.CostEstimate(flops=0, bytes_accessed=2 << 20, transcendentals=0),
        name="stack",
    )(*values, *waited)


def pages_kernel(facts_ref, *refs):
    kept_refs, given_ref, out_ref, turned_ref = refs[:4], refs[4], refs[5], refs[6]
    blocks = facts_ref.shape[0] - LAST - out_ref.shape[1]
    chip, core = facts_ref[CHIP], facts_ref[CORE]
    for tile in range(given_ref.shape[2] // 128):
        tokens = slice(tile * 128, (tile + 1) * 128)
        for kind in range(2):
            entries = slice((kind + 1) * HD, (kind + 2) * HD)
            for distance in range(4):
                head = 2 * (chip ^ distance)
                turned_ref[head + core] = kept_refs[distance][entries, tokens]
                turned_ref[head + 1 - core] = given_ref[distance, entries, tokens]
            turned = turned_ref[...].reshape(8 * HD, 128).T
            for page in range(128 // PAGE):
                place = facts_ref[LAST + blocks + tile * 128 // PAGE + page]
                out_ref[kind, place] = turned[page * PAGE : (page + 1) * PAGE]


def pages(facts, count, parts):
    width = 8 * HD
    vmem = pl.BlockSpec(memory_space=pltpu.VMEM)
    return pl.pallas_call(
        pages_kernel,
        in_specs=[pl.BlockSpec(memory_space=pltpu.SMEM)] + [vmem] * len(parts),
        out_specs=vmem,
        scratch_shapes=[pltpu.VMEM((8, HD, 128), jnp.bfloat16)],
        out_shape=jax.ShapeDtypeStruct((2, count, PAGE, width), jnp.bfloat16),
        compiler_params=pltpu.CompilerParams(vmem_limit_bytes=56 << 20),
        cost_estimate=pl.CostEstimate(flops=0, bytes_accessed=10 << 20, transcendentals=0),
        name="pages",
    )(facts, *parts)


def per_device_heads(hidden_in, ln_gain, w_qkv, w_out, doc_lengths, segment_ids, pair_table, page_table):
    rows, depth = hidden_in.shape
    width = w_qkv.shape[2]
    block, place = lax.axis_index("blk"), lax.axis_index("tp")
    chip = block // 2
    blocks = lax.axis_size("blk")
    values32 = hidden_in.astype(jnp.float32)
    own_mean = jnp.mean(values32, axis=1)
    own_square = jnp.mean((values32 - own_mean[:, None]) ** 2, axis=1)
    own_stats = jnp.stack([own_mean, own_square])
    stats = jnp.stack([own_stats] + [turn(own_stats, distance) for distance in (1, 2, 3)])
    mean = jnp.mean(stats[:, 0], axis=0)
    variance = jnp.mean(stats[:, 1] + (stats[:, 0] - mean[None]) ** 2, axis=0)
    rstd = lax.rsqrt(variance + EPSILON)[:, None]
    mean = mean[:, None]
    gain = ln_gain.reshape(4, 1, depth)
    w3 = jnp.transpose(w_qkv, (1, 0, 2))

    token_index = block * rows + jnp.arange(rows, dtype=jnp.int32)
    positions = doc_positions(token_index, doc_lengths, segment_ids)
    frequency = 10000.0 ** (-(2.0 * jnp.arange(ROT // 2, dtype=jnp.float32)) / ROT)
    angles = positions.astype(jnp.float32)[None, :] * frequency[:, None]
    cosine, sine = jnp.cos(angles), jnp.sin(angles)
    cosine = jnp.concatenate([cosine, cosine])
    sine = jnp.concatenate([-sine, sine])

    ends = jnp.cumsum(doc_lengths)
    tokens = jnp.arange(blocks * rows, dtype=jnp.int32)
    start = jnp.max(jnp.where(ends[:, None] <= tokens[None, :], ends[:, None], 0), axis=0)
    start = start.astype(jnp.int32).reshape(blocks, 1, rows)
    page_count = rows // PAGE
    steps = line_owners()
    numbers = [owner for owner, _ in steps] + [pick for _, pick in steps]
    numbers += [jnp.maximum((place - owner) % 4 - 1, 0) for owner, _ in steps] + [chip, block % 2]
    facts = jnp.concatenate(
        [
            jnp.stack([jnp.asarray(number).astype(jnp.int32) for number in numbers]),
            start[:, 0, rows - 1],
            page_table - block * page_count,
        ]
    )

    windows = jnp.stack([block] + [(place + distance) % 4 for distance in (1, 2, 3)]).astype(jnp.int32)
    windows = shares(windows, w_out, depth)
    windows = list(windows)
    total = [None]

    def take_in(step, arrays):
        total[0] = project(
            step, facts, arrays, mean, rstd, gain, w3, total[0], [cosine, sine], windows
        )

    gather_line(hidden_in, take_in)
    *kept, given = total[0]
    arrived = to_heads(kept, swap(given, 1))
    page_cache = pages(facts, page_count, [*kept, given])

    columns = [turn(window, distance) for distance, window in zip((1, 2, 3), windows)]
    mixed = list(attend(facts, pair_table, start, arrived))
    others = lax.all_gather(stack(columns, mixed[:1]), "blk", axis=0)
    heads = to_blocks(facts, mixed)

    came, result = [], [None]

    def add_in(step, arrays):
        came.append(arrays)
        if step == 2:
            result[0] = combine((0, 1, 2), facts, came[:3], w_out, others)
        if step == 3:
            result[0] = combine((3,), facts, came[3:], None, others, result[0])

    gather_line(heads, add_in)
    attn_out = result[0]
    return (attn_out, page_cache)


def solution(mesh):
    placed = (P("blk", "tp"), P(), P(None, None, "tp"), P("tp", None), P(), P("blk"), P(), P("blk"))

    def per_device(hidden_in, ln_gain, w_qkv, *rest):
        heads = w_qkv.shape[2] // HD
        fits = mesh.shape["tp"] == 4 and mesh.shape["blk"] == 8 and heads == 8
        form = per_device_heads if fits else per_device_any
        return form(hidden_in, ln_gain, w_qkv, *rest)

    return jax.shard_map(
        per_device,
        mesh=mesh,
        in_specs=placed,
        out_specs=(P("blk", "tp"), P(None, "blk", None, "tp")),
        check_vma=False,
    )
```

```python
import functools

import jax
import jax.numpy as jnp
from jax import lax
from jax.experimental import pallas as pl
from jax.experimental.pallas import tpu as pltpu
from jax.sharding import PartitionSpec as P

HD = 96
ROT = 24
PAGE = 16


EPSILON = 1e-05
QUERY_SCALE = HD ** (-0.5) * 1.4426950408889634


def from_behind(value, axis, steps):
    count = lax.axis_size(axis)
    first, last = (max(0, -steps), min(count, count - steps))
    return lax.ppermute(value, axis, [(source, source + steps) for source in range(first, last)])


def layer_norm(whole, ln_gain):
    values32 = whole.astype(jnp.float32)
    row_mean = jnp.mean(values32, axis=-1, keepdims=True)
    centred = values32 - row_mean
    row_var = jnp.mean(centred * centred, axis=-1, keepdims=True)
    return (centred * lax.rsqrt(row_var + EPSILON) * ln_gain).astype(jnp.bfloat16)


def doc_positions(token_index, doc_lengths, segment_ids):
    starts = jnp.cumsum(doc_lengths) - doc_lengths
    slots = jnp.arange(doc_lengths.shape[0], dtype=jnp.int32)
    in_document = segment_ids[:, None] == slots[None, :]
    offsets = jnp.sum(jnp.where(in_document, starts[None, :], 0), axis=1)
    return token_index - offsets


def rotary(head_block, positions):
    half_rot = ROT // 2
    frequency = 10000.0 ** (-(2.0 * jnp.arange(half_rot, dtype=jnp.float32)) / ROT)
    angles = positions.astype(jnp.float32)[:, None] * frequency[None, :]
    cosine = jnp.cos(angles)[:, None, :]
    sine_part = jnp.sin(angles)[:, None, :]
    lower_half = head_block[..., :half_rot]
    upper_half = head_block[..., half_rot:ROT]
    return jnp.concatenate(
        [
            lower_half * cosine - upper_half * sine_part,
            upper_half * cosine + lower_half * sine_part,
            head_block[..., ROT:],
        ],
        axis=-1,
    )


def per_device_any(hidden_in, ln_gain, w_qkv, w_out, doc_lengths, segment_ids, pair_table, page_table):
    row_count = hidden_in.shape[0]
    whole = lax.all_gather(hidden_in, "tp", axis=1, tiled=True)
    normed = layer_norm(whole, ln_gain)
    col_count = w_qkv.shape[2]
    head_count = col_count // HD
    projected = jnp.einsum("tk,kcn->ctn", normed, w_qkv, preferred_element_type=jnp.float32)
    projected = projected.reshape(3, row_count, head_count, HD)
    block_index = lax.axis_index("blk")
    token_index = block_index * row_count + jnp.arange(row_count, dtype=jnp.int32)
    positions = doc_positions(token_index, doc_lengths, segment_ids)
    queries = rotary(projected[0], positions).astype(jnp.bfloat16)
    key_rows = rotary(projected[1], positions).astype(jnp.bfloat16)
    values = projected[2].astype(jnp.bfloat16)
    table_row = lax.dynamic_index_in_dim(pair_table, block_index, 0, keepdims=False)
    block_ids = jnp.arange(pair_table.shape[1], dtype=jnp.int32)
    scale = HD ** (-0.5)

    def attend(running, incoming, offset):
        key_piece, value_piece, segment_piece = incoming
        piece_rows = key_piece.shape[0]
        key_index = offset + jnp.arange(piece_rows, dtype=jnp.int32)
        matches = (key_index // row_count)[:, None] == block_ids[None, :]
        live = jnp.sum(jnp.where(matches, table_row[None, :], 0), axis=1) > 0

        def compute(previous):
            maxima, totals, weighted = previous
            scores = (
                jnp.einsum("qhd,khd->hqk", queries, key_piece, preferred_element_type=jnp.float32)
                * scale
            )
            allowed = (
                live[None, :]
                & (segment_ids[:, None] == segment_piece[None, :])
                & (key_index[None, :] <= token_index[:, None])
            )
            scores = jnp.where(allowed[None], scores, -jnp.inf)
            newest = jnp.maximum(maxima, jnp.max(scores, axis=-1))
            shrink = jnp.exp(maxima - newest)
            weights = jnp.exp(scores - newest[..., None])
            totals = totals * shrink + jnp.sum(weights, axis=-1)
            weighted = weighted * shrink[..., None] + jnp.einsum(
                "hqk,khd->hqd",
                weights.astype(jnp.bfloat16),
                value_piece,
                preferred_element_type=jnp.float32,
            )
            return (newest, totals, weighted)

        return lax.cond(jnp.any(live), compute, lambda previous: previous, running)

    start_state = (
        jnp.full((head_count, row_count), -1e30, jnp.float32),
        jnp.zeros((head_count, row_count), jnp.float32),
        jnp.zeros((head_count, row_count, HD), jnp.float32),
    )
    final = attend(start_state, (key_rows, values, segment_ids), block_index * row_count)
    for distance in range(1, lax.axis_size("blk") // 2 + 1):
        earlier = from_behind((key_rows, values, segment_ids), "blk", distance)
        final = attend(final, earlier, (block_index - distance) * row_count)
    mixed = (final[2] / final[1][..., None]).astype(jnp.bfloat16)
    heads_out = jnp.transpose(mixed, (1, 0, 2)).reshape(row_count, col_count)
    partial_term = jnp.dot(heads_out, w_out, preferred_element_type=jnp.float32)
    attn_out = lax.psum_scatter(
        partial_term.astype(jnp.bfloat16), "tp", scatter_dimension=1, tiled=True
    )
    page_count = row_count // PAGE
    local_pages = page_table - block_index * page_count
    stacked = jnp.stack(
        [key_rows.reshape(page_count, PAGE, col_count), values.reshape(page_count, PAGE, col_count)]
    )
    page_cache = jnp.zeros_like(stacked).at[:, local_pages].set(stacked)
    return (attn_out, page_cache)


def turn(value, distance):
    return lax.ppermute(value, "tp", [(source, (source + distance) % 4) for source in range(4)])


def line_hop(up, down, ups, downs):
    return lax.ppermute(up, "tp", ups), lax.ppermute(down, "tp", downs)


def line_owners():
    place = lax.axis_index("tp")
    first = jnp.where(place == 0, 1, place - 1)
    second = jnp.where(place == 0, 2, jnp.where(place == 3, 1, place + 1))
    third = jnp.where(place < 2, 3, 0)
    pick_second = jnp.where(place == 0, 1, jnp.where(place == 3, 2, 0))
    outer = (place == 0) | (place == 3)
    return [(place, 0 * place), (first, place == 0), (second, pick_second), (third, outer)]


def gather_line(value, work):
    up1, down1 = line_hop(value, value, [(0, 1), (1, 2), (2, 3)], [(3, 2), (2, 1), (1, 0)])
    work(0, [value])
    up2, down2 = line_hop(up1, down1, [(1, 2), (2, 3)], [(2, 1), (1, 0)])
    work(1, [up1, down1])
    inner = jnp.where(lax.axis_index("tp") == 2, up2, down2)
    outer = lax.ppermute(inner, "tp", [(2, 3), (1, 0)])
    work(2, [down1, down2, up2])
    work(3, [inner, outer])


OWNER, PICK, COLUMN, CHIP, CORE, LAST = 0, 4, 8, 12, 13, 14


def project_kernel(step, count, facts_ref, *refs):
    refs = list(refs)
    shards = refs[:count]
    mean_ref, rstd_ref, gain_ref, w_ref = refs[count : count + 4]
    del refs[: count + 4]
    previous_ref = refs.pop(0) if step > 0 else None
    kind = pl.program_id(0)
    normed_ref, turned_ref = refs[-2:]

    for pick, x_ref in enumerate(shards):

        @pl.when((kind == 0) & (facts_ref[PICK + step] == pick))
        def _():
            centred = x_ref[...].astype(jnp.float32) - mean_ref[...]
            normed_ref[...] = (centred * rstd_ref[...] * gain_ref[0]).astype(jnp.bfloat16)

    total = jnp.dot(normed_ref[...], w_ref[0], preferred_element_type=jnp.float32)
    if step > 0:
        total = total + previous_ref[0]
    if step < 3:
        refs[0][0] = total
        return
    cos_ref, sin_ref = refs[:2]
    kept_refs, given_ref = refs[5:9], refs[9]
    chip, core = facts_ref[CHIP], facts_ref[CORE]
    turned = total.T * jnp.where(kind == 0, QUERY_SCALE, 1.0)
    turned_ref[...] = turned.reshape(turned_ref.shape).astype(jnp.bfloat16)

    @pl.when(kind < 2)
    def _():
        half = ROT // 2
        for head in range(turned_ref.shape[0]):
            part = turned[head * HD : head * HD + ROT]
            swapped = jnp.concatenate([part[half:], part[:half]], axis=0)
            turned_ref[head, :ROT] = (part * cos_ref[...] + swapped * sin_ref[...]).astype(jnp.bfloat16)

    for distance in range(4):
        head = 2 * (chip ^ distance)
        kept_refs[distance][...] = turned_ref[head + core]
        given_ref[distance] = turned_ref[head + 1 - core]


def project(step, facts, shards, mean, rstd, gain, w3, previous, tables, waited):
    rows, depth = shards[0].shape
    width = w3.shape[2]
    column = pl.BlockSpec((rows, 1), lambda c, o: (0, 0))
    in_specs = [pl.BlockSpec((rows, depth), lambda c, o: (0, 0)) for _ in shards] + [
        column,
        column,
        pl.BlockSpec((1, 1, depth), lambda c, o: (o[OWNER + step], 0, 0)),
        pl.BlockSpec((1, depth, width), lambda c, o: (c, o[OWNER + step], 0)),
    ]
    args = [*shards, mean, rstd, gain, w3]
    sums = pl.BlockSpec((1, rows, width), lambda c, o: (c, 0, 0))
    if step > 0:
        in_specs.append(sums)
        args.append(previous)
    out_shape, out_specs = jax.ShapeDtypeStruct((3, rows, width), jnp.float32), sums
    if step == 3:
        in_specs += [pl.BlockSpec((ROT, rows), lambda c, o: (0, 0))] * 2
        in_specs += [pl.BlockSpec(memory_space=pl.ANY)] * len(waited)
        args += tables + waited
        out_shape = [jax.ShapeDtypeStruct((3 * HD, rows), jnp.bfloat16)] * 4
        out_shape.append(jax.ShapeDtypeStruct((4, 3 * HD, rows), jnp.bfloat16))
        out_specs = [pl.BlockSpec((HD, rows), lambda c, o: (c, 0))] * 4
        out_specs.append(pl.BlockSpec((4, HD, rows), lambda c, o: (0, c, 0)))
    return pl.pallas_call(
        functools.partial(project_kernel, step, len(shards)),
        grid_spec=pltpu.PrefetchScalarGridSpec(
            num_scalar_prefetch=1,
            grid=(3,),
            in_specs=in_specs,
            out_specs=out_specs,
            scratch_shapes=[
                pltpu.VMEM((rows, depth), jnp.bfloat16),
                pltpu.VMEM((width // HD, HD, rows), jnp.bfloat16),
            ],
        ),
        out_shape=out_shape,
        compiler_params=pltpu.CompilerParams(vmem_limit_bytes=48 << 20),
        cost_estimate=pl.CostEstimate(
            flops=(1, 20, 20, 6)[step] * rows * depth * width, bytes_accessed=0, transcendentals=0
        ),
        name="project",
    )(facts, *args)


def attend_kernel(facts_ref, pair_ref, start_ref, *refs):
    pieces, outs, (q_ref, k_ref, v_ref, top_ref, sum_ref, acc_ref) = refs[:-10], refs[-10:-6], refs[-6:]
    chip, own_core = facts_ref[CHIP], facts_ref[CORE]
    rows = q_ref.shape[2]
    for distance in range(4):
        for other, piece in enumerate(pieces[2 * distance : 2 * distance + 2]):
            block = 2 * (chip ^ distance) + (own_core ^ other)
            q_ref[block] = piece[:HD]
            k_ref[block] = piece[HD : 2 * HD].T
            v_ref[block] = piece[2 * HD :]
    def one_block(block, carry):
        token = block * rows + lax.broadcasted_iota(jnp.int32, (1, rows), 1)
        start = start_ref[block]
        top_ref[...] = jnp.full_like(top_ref, -1e30)
        sum_ref[...] = jnp.zeros_like(sum_ref)
        acc_ref[...] = jnp.zeros_like(acc_ref)

        def update(other, masked):
            scores = jnp.dot(k_ref[other], q_ref[block], preferred_element_type=jnp.float32)
            if masked:
                key = other * rows + lax.broadcasted_iota(jnp.int32, (rows, rows), 0)
                scores = jnp.where((key >= start) & (key <= token), scores, -jnp.inf)
            newest = jnp.maximum(top_ref[...], jnp.max(scores, axis=0, keepdims=True))
            shrink = jnp.exp2(top_ref[...] - newest)
            weights = jnp.exp2(scores - newest)
            top_ref[...] = newest
            sum_ref[...] = sum_ref[...] * shrink + jnp.sum(weights, axis=0, keepdims=True)
            acc_ref[...] = acc_ref[...] * shrink + jnp.dot(
                v_ref[other], weights.astype(jnp.bfloat16), preferred_element_type=jnp.float32
            )

        def one_pair(other, inner):
            live = pair_ref[block, other] > 0
            whole = facts_ref[LAST + block] <= other * rows

            @pl.when(live & whole & (other < block))
            def _():
                update(other, False)

            @pl.when(live & ~(whole & (other < block)))
            def _():
                update(other, True)

            return inner

        lax.fori_loop(0, block + 1, one_pair, 0)
        mixed = (acc_ref[...] / sum_ref[...]).astype(jnp.bfloat16)
        for distance, out_ref in enumerate(outs):

            @pl.when((block // 2) ^ chip == distance)
            def _():
                out_ref[block % 2] = mixed

        return carry

    lax.fori_loop(0, q_ref.shape[0], one_block, 0)


def attend(facts, pair_table, start, pieces):
    blocks, _, rows = start.shape
    smem = pl.BlockSpec(memory_space=pltpu.SMEM)
    vmem = pl.BlockSpec(memory_space=pltpu.VMEM)
    return pl.pallas_call(
        attend_kernel,
        in_specs=[smem, smem, vmem] + [vmem] * len(pieces),
        out_specs=[vmem] * 4,
        out_shape=[jax.ShapeDtypeStruct((2, HD, rows), jnp.bfloat16)] * 4,
        scratch_shapes=[
            pltpu.VMEM((blocks, HD, rows), jnp.bfloat16),
            pltpu.VMEM((blocks, rows, HD), jnp.bfloat16),
            pltpu.VMEM((blocks, HD, rows), jnp.bfloat16),
            pltpu.VMEM((1, rows), jnp.float32),
            pltpu.VMEM((1, rows), jnp.float32),
            pltpu.VMEM((HD, rows), jnp.float32),
        ],
        compiler_params=pltpu.CompilerParams(vmem_limit_bytes=28 << 20),
        cost_estimate=pl.CostEstimate(flops=1000, bytes_accessed=1000, transcendentals=0),
        name="attend",
    )(facts, pair_table, start, *pieces)


def swap(value, distance):
    count = lax.axis_size("blk")
    return lax.ppermute(value, "blk", [(place, place ^ distance) for place in range(count)])


def to_heads(kept, got):
    pieces = []
    for distance in range(4):
        for value in (kept[distance], got[distance]):
            pieces.append(value if distance == 0 else swap(value, 2 * distance))
    return pieces


def order_kernel(facts_ref, *refs):
    pairs, got_ref, out_ref = refs[:4], refs[4], refs[5]
    chip, core = facts_ref[CHIP], facts_ref[CORE]
    for distance in range(4):
        head = 2 * (chip ^ distance)
        out_ref[head + core] = pairs[distance][core]
        out_ref[head + 1 - core] = got_ref[distance]


def to_blocks(facts, mixed):
    core = lax.axis_index("blk") % 2
    held = mixed[:1] + [swap(mixed[distance], 2 * distance) for distance in (1, 2, 3)]
    given = [lax.dynamic_index_in_dim(pair, 1 - core, 0, keepdims=False) for pair in held]
    got = swap(jnp.stack(given), 1)
    vmem = pl.BlockSpec(memory_space=pltpu.VMEM)
    heads = pl.pallas_call(
        order_kernel,
        in_specs=[pl.BlockSpec(memory_space=pltpu.SMEM)] + [vmem] * 5,
        out_specs=vmem,
        out_shape=jax.ShapeDtypeStruct((8,) + got.shape[1:], got.dtype),
        cost_estimate=pl.CostEstimate(flops=0, bytes_accessed=2 << 20, transcendentals=0),
        name="order",
    )(facts, *held, got)
    return heads.reshape((8 * HD,) + got.shape[2:])


def combine_kernel(steps, counts, facts_ref, *refs):
    refs = list(refs)
    arrays = []
    for count in counts:
        arrays.append(refs[:count])
        del refs[:count]
    own_ref, others_ref = (refs.pop(0) if 0 in steps else None), refs.pop(0)
    previous_ref = refs.pop(0) if 0 not in steps else None
    out_ref, sum_ref = refs
    slot = pl.program_id(1)
    for place, step in enumerate(steps):
        for pick, h_ref in enumerate(arrays[place]):

            @pl.when((slot == place) & (facts_ref[PICK + step] == pick))
            def _():
                w_ref = own_ref if step == 0 else others_ref
                product = lax.dot_general(
                    h_ref[...],
                    w_ref[...].reshape(h_ref.shape[0], out_ref.shape[1]),
                    (((0,), (0,)), ((), ())),
                    preferred_element_type=jnp.float32,
                )
                if place > 0:
                    product = product + sum_ref[...]
                elif previous_ref is not None:
                    product = product + previous_ref[...].astype(jnp.float32)
                if place < len(steps) - 1:
                    sum_ref[...] = product
                else:
                    out_ref[...] = product.astype(out_ref.dtype)


def combine(steps, facts, arrays, own, others, previous=None):
    depth, rows = arrays[-1][-1].shape
    outer, _, inner, width = others.shape
    tile = width // 2
    out_spec = pl.BlockSpec((rows, tile), lambda n, k, o: (0, n))
    in_specs = [pl.BlockSpec((depth, rows), lambda n, k, o: (0, 0)) for step in arrays for _ in step]
    args = [array for step in arrays for array in step]
    if 0 in steps:
        in_specs.append(
            pl.BlockSpec((depth, tile), lambda n, k, o: (0, o[OWNER] * (width // tile) + n))
        )
        args.append(own)
    in_specs.append(
        pl.BlockSpec((outer, 1, inner, tile), lambda n, k, o: (0, o[COLUMN + steps[0] + k], 0, n))
    )
    args.append(others)
    if 0 not in steps:
        in_specs.append(out_spec)
        args.append(previous)
    return pl.pallas_call(
        functools.partial(combine_kernel, steps, tuple(len(step) for step in arrays)),
        grid_spec=pltpu.PrefetchScalarGridSpec(
            num_scalar_prefetch=1,
            grid=(width // tile, len(steps)),
            in_specs=in_specs,
            out_specs=out_spec,
            scratch_shapes=[pltpu.VMEM((rows, tile), jnp.float32)],
        ),
        out_shape=jax.ShapeDtypeStruct((rows, width), jnp.bfloat16),
        compiler_params=pltpu.CompilerParams(vmem_limit_bytes=56 << 20),
        cost_estimate=pl.CostEstimate(
            flops=4 * len(steps) * rows * depth * width,
            bytes_accessed=2 * len(steps) * depth * width,
            transcendentals=0,
        ),
        name="combine",
    )(facts, *args)


def share_kernel(facts_ref, w_ref, *refs):
    outs, sems = refs[:3], refs[3]
    rows, width = outs[0].shape
    first = facts_ref[0] * rows
    copies = []
    for place, out_ref in enumerate(outs):
        begin = pl.multiple_of(facts_ref[1 + place] * width, width)
        window = w_ref.at[pl.ds(pl.multiple_of(first, rows), rows), pl.ds(begin, width)]
        copies.append(pltpu.make_async_copy(window, out_ref, sems.at[place]))
    for copy in copies:
        copy.start()
    for copy in copies:
        copy.wait()


def shares(numbers, w_out, width):
    any_space = pl.BlockSpec(memory_space=pl.ANY)
    return pl.pallas_call(
        share_kernel,
        in_specs=[pl.BlockSpec(memory_space=pltpu.SMEM), any_space],
        out_specs=[pl.BlockSpec(memory_space=pltpu.VMEM)] * 3,
        out_shape=[jax.ShapeDtypeStruct((HD, width), w_out.dtype)] * 3,
        scratch_shapes=[pltpu.SemaphoreType.DMA((3,))],
        cost_estimate=pl.CostEstimate(flops=0, bytes_accessed=2 << 20, transcendentals=0),
        name="shares",
    )(numbers, w_out)


def stack_kernel(*refs):
    for place in range(3):
        refs[-1][place] = refs[place][...]


def stack(values, waited):
    any_space, vmem = pl.BlockSpec(memory_space=pl.ANY), pl.BlockSpec(memory_space=pltpu.VMEM)
    return pl.pallas_call(
        stack_kernel,
        in_specs=[vmem] * 3 + [any_space] * len(waited),
        out_specs=vmem,
        out_shape=jax.ShapeDtypeStruct((3,) + values[0].shape, values[0].dtype),
        cost_estimate=pl.CostEstimate(flops=0, bytes_accessed=2 << 20, transcendentals=0),
        name="stack",
    )(*values, *waited)


def pages_kernel(facts_ref, *refs):
    kept_refs, given_ref, out_ref, turned_ref = refs[:4], refs[4], refs[5], refs[6]
    blocks = facts_ref.shape[0] - LAST - out_ref.shape[1]
    chip, core = facts_ref[CHIP], facts_ref[CORE]
    for tile in range(given_ref.shape[2] // 128):
        tokens = slice(tile * 128, (tile + 1) * 128)
        for kind in range(2):
            entries = slice((kind + 1) * HD, (kind + 2) * HD)
            for distance in range(4):
                head = 2 * (chip ^ distance)
                turned_ref[head + core] = kept_refs[distance][entries, tokens]
                turned_ref[head + 1 - core] = given_ref[distance, entries, tokens]
            turned = turned_ref[...].reshape(8 * HD, 128).T
            for page in range(128 // PAGE):
                place = facts_ref[LAST + blocks + tile * 128 // PAGE + page]
                out_ref[kind, place] = turned[page * PAGE : (page + 1) * PAGE]


def pages(facts, count, parts):
    width = 8 * HD
    vmem = pl.BlockSpec(memory_space=pltpu.VMEM)
    return pl.pallas_call(
        pages_kernel,
        in_specs=[pl.BlockSpec(memory_space=pltpu.SMEM)] + [vmem] * len(parts),
        out_specs=vmem,
        scratch_shapes=[pltpu.VMEM((8, HD, 128), jnp.bfloat16)],
        out_shape=jax.ShapeDtypeStruct((2, count, PAGE, width), jnp.bfloat16),
        compiler_params=pltpu.CompilerParams(vmem_limit_bytes=56 << 20),
        cost_estimate=pl.CostEstimate(flops=0, bytes_accessed=10 << 20, transcendentals=0),
        name="pages",
    )(facts, *parts)


def per_device_heads(hidden_in, ln_gain, w_qkv, w_out, doc_lengths, segment_ids, pair_table, page_table):
    rows, depth = hidden_in.shape
    width = w_qkv.shape[2]
    block, place = lax.axis_index("blk"), lax.axis_index("tp")
    chip = block // 2
    blocks = lax.axis_size("blk")
    values32 = hidden_in.astype(jnp.float32)
    own_mean = jnp.mean(values32, axis=1)
    own_square = jnp.mean((values32 - own_mean[:, None]) ** 2, axis=1)
    own_stats = jnp.stack([own_mean, own_square])
    stats = jnp.stack([own_stats] + [turn(own_stats, distance) for distance in (1, 2, 3)])
    mean = jnp.mean(stats[:, 0], axis=0)
    variance = jnp.mean(stats[:, 1] + (stats[:, 0] - mean[None]) ** 2, axis=0)
    rstd = lax.rsqrt(variance + EPSILON)[:, None]
    mean = mean[:, None]
    gain = ln_gain.reshape(4, 1, depth)
    w3 = jnp.transpose(w_qkv, (1, 0, 2))

    token_index = block * rows + jnp.arange(rows, dtype=jnp.int32)
    positions = doc_positions(token_index, doc_lengths, segment_ids)
    frequency = 10000.0 ** (-(2.0 * jnp.arange(ROT // 2, dtype=jnp.float32)) / ROT)
    angles = positions.astype(jnp.float32)[None, :] * frequency[:, None]
    cosine, sine = jnp.cos(angles), jnp.sin(angles)
    cosine = jnp.concatenate([cosine, cosine])
    sine = jnp.concatenate([-sine, sine])

    ends = jnp.cumsum(doc_lengths)
    tokens = jnp.arange(blocks * rows, dtype=jnp.int32)
    start = jnp.max(jnp.where(ends[:, None] <= tokens[None, :], ends[:, None], 0), axis=0)
    start = start.astype(jnp.int32).reshape(blocks, 1, rows)
    page_count = rows // PAGE
    steps = line_owners()
    numbers = [owner for owner, _ in steps] + [pick for _, pick in steps]
    numbers += [jnp.maximum((place - owner) % 4 - 1, 0) for owner, _ in steps] + [chip, block % 2]
    facts = jnp.concatenate(
        [
            jnp.stack([jnp.asarray(number).astype(jnp.int32) for number in numbers]),
            start[:, 0, rows - 1],
            page_table - block * page_count,
        ]
    )

    windows = jnp.stack([block] + [(place + distance) % 4 for distance in (1, 2, 3)]).astype(jnp.int32)
    windows = shares(windows, w_out, depth)
    windows = list(windows)
    total = [None]

    def take_in(step, arrays):
        total[0] = project(
            step, facts, arrays, mean, rstd, gain, w3, total[0], [cosine, sine], windows
        )

    gather_line(hidden_in, take_in)
    *kept, given = total[0]
    arrived = to_heads(kept, swap(given, 1))
    page_cache = pages(facts, page_count, [*kept, given])

    columns = [turn(window, distance) for distance, window in zip((1, 2, 3), windows)]
    mixed = list(attend(facts, pair_table, start, arrived))
    heads = to_blocks(facts, mixed)
    others = lax.all_gather(stack(columns, [heads]), "blk", axis=0)

    came, result = [], [None]

    def add_in(step, arrays):
        came.append(arrays)
        if step == 2:
            result[0] = combine((0, 1, 2), facts, came[:3], w_out, others)
        if step == 3:
            result[0] = combine((3,), facts, came[3:], None, others, result[0])

    gather_line(heads, add_in)
    attn_out = result[0]
    return (attn_out, page_cache)


def solution(mesh):
    placed = (P("blk", "tp"), P(), P(None, None, "tp"), P("tp", None), P(), P("blk"), P(), P("blk"))

    def per_device(hidden_in, ln_gain, w_qkv, *rest):
        heads = w_qkv.shape[2] // HD
        fits = mesh.shape["tp"] == 4 and mesh.shape["blk"] == 8 and heads == 8
        form = per_device_heads if fits else per_device_any
        return form(hidden_in, ln_gain, w_qkv, *rest)

    return jax.shard_map(
        per_device,
        mesh=mesh,
        in_specs=placed,
        out_specs=(P("blk", "tp"), P(None, "blk", None, "tp")),
        check_vma=False,
    )
```

```python
import functools

import jax
import jax.numpy as jnp
from jax import lax
from jax.experimental import pallas as pl
from jax.experimental.pallas import tpu as pltpu
from jax.sharding import PartitionSpec as P

HD = 96
ROT = 24
PAGE = 16


EPSILON = 1e-05
QUERY_SCALE = HD ** (-0.5) * 1.4426950408889634


def from_behind(value, axis, steps):
    count = lax.axis_size(axis)
    first, last = (max(0, -steps), min(count, count - steps))
    return lax.ppermute(value, axis, [(source, source + steps) for source in range(first, last)])


def layer_norm(whole, ln_gain):
    values32 = whole.astype(jnp.float32)
    row_mean = jnp.mean(values32, axis=-1, keepdims=True)
    centred = values32 - row_mean
    row_var = jnp.mean(centred * centred, axis=-1, keepdims=True)
    return (centred * lax.rsqrt(row_var + EPSILON) * ln_gain).astype(jnp.bfloat16)


def doc_positions(token_index, doc_lengths, segment_ids):
    starts = jnp.cumsum(doc_lengths) - doc_lengths
    slots = jnp.arange(doc_lengths.shape[0], dtype=jnp.int32)
    in_document = segment_ids[:, None] == slots[None, :]
    offsets = jnp.sum(jnp.where(in_document, starts[None, :], 0), axis=1)
    return token_index - offsets


def rotary(head_block, positions):
    half_rot = ROT // 2
    frequency = 10000.0 ** (-(2.0 * jnp.arange(half_rot, dtype=jnp.float32)) / ROT)
    angles = positions.astype(jnp.float32)[:, None] * frequency[None, :]
    cosine = jnp.cos(angles)[:, None, :]
    sine_part = jnp.sin(angles)[:, None, :]
    lower_half = head_block[..., :half_rot]
    upper_half = head_block[..., half_rot:ROT]
    return jnp.concatenate(
        [
            lower_half * cosine - upper_half * sine_part,
            upper_half * cosine + lower_half * sine_part,
            head_block[..., ROT:],
        ],
        axis=-1,
    )


def per_device_any(hidden_in, ln_gain, w_qkv, w_out, doc_lengths, segment_ids, pair_table, page_table):
    row_count = hidden_in.shape[0]
    whole = lax.all_gather(hidden_in, "tp", axis=1, tiled=True)
    normed = layer_norm(whole, ln_gain)
    col_count = w_qkv.shape[2]
    head_count = col_count // HD
    projected = jnp.einsum("tk,kcn->ctn", normed, w_qkv, preferred_element_type=jnp.float32)
    projected = projected.reshape(3, row_count, head_count, HD)
    block_index = lax.axis_index("blk")
    token_index = block_index * row_count + jnp.arange(row_count, dtype=jnp.int32)
    positions = doc_positions(token_index, doc_lengths, segment_ids)
    queries = rotary(projected[0], positions).astype(jnp.bfloat16)
    key_rows = rotary(projected[1], positions).astype(jnp.bfloat16)
    values = projected[2].astype(jnp.bfloat16)
    table_row = lax.dynamic_index_in_dim(pair_table, block_index, 0, keepdims=False)
    block_ids = jnp.arange(pair_table.shape[1], dtype=jnp.int32)
    scale = HD ** (-0.5)

    def attend(running, incoming, offset):
        key_piece, value_piece, segment_piece = incoming
        piece_rows = key_piece.shape[0]
        key_index = offset + jnp.arange(piece_rows, dtype=jnp.int32)
        matches = (key_index // row_count)[:, None] == block_ids[None, :]
        live = jnp.sum(jnp.where(matches, table_row[None, :], 0), axis=1) > 0

        def compute(previous):
            maxima, totals, weighted = previous
            scores = (
                jnp.einsum("qhd,khd->hqk", queries, key_piece, preferred_element_type=jnp.float32)
                * scale
            )
            allowed = (
                live[None, :]
                & (segment_ids[:, None] == segment_piece[None, :])
                & (key_index[None, :] <= token_index[:, None])
            )
            scores = jnp.where(allowed[None], scores, -jnp.inf)
            newest = jnp.maximum(maxima, jnp.max(scores, axis=-1))
            shrink = jnp.exp(maxima - newest)
            weights = jnp.exp(scores - newest[..., None])
            totals = totals * shrink + jnp.sum(weights, axis=-1)
            weighted = weighted * shrink[..., None] + jnp.einsum(
                "hqk,khd->hqd",
                weights.astype(jnp.bfloat16),
                value_piece,
                preferred_element_type=jnp.float32,
            )
            return (newest, totals, weighted)

        return lax.cond(jnp.any(live), compute, lambda previous: previous, running)

    start_state = (
        jnp.full((head_count, row_count), -1e30, jnp.float32),
        jnp.zeros((head_count, row_count), jnp.float32),
        jnp.zeros((head_count, row_count, HD), jnp.float32),
    )
    final = attend(start_state, (key_rows, values, segment_ids), block_index * row_count)
    for distance in range(1, lax.axis_size("blk") // 2 + 1):
        earlier = from_behind((key_rows, values, segment_ids), "blk", distance)
        final = attend(final, earlier, (block_index - distance) * row_count)
    mixed = (final[2] / final[1][..., None]).astype(jnp.bfloat16)
    heads_out = jnp.transpose(mixed, (1, 0, 2)).reshape(row_count, col_count)
    partial_term = jnp.dot(heads_out, w_out, preferred_element_type=jnp.float32)
    attn_out = lax.psum_scatter(
        partial_term.astype(jnp.bfloat16), "tp", scatter_dimension=1, tiled=True
    )
    page_count = row_count // PAGE
    local_pages = page_table - block_index * page_count
    stacked = jnp.stack(
        [key_rows.reshape(page_count, PAGE, col_count), values.reshape(page_count, PAGE, col_count)]
    )
    page_cache = jnp.zeros_like(stacked).at[:, local_pages].set(stacked)
    return (attn_out, page_cache)


def turn(value, distance):
    return lax.ppermute(value, "tp", [(source, (source + distance) % 4) for source in range(4)])


def line_hop(up, down, ups, downs):
    return lax.ppermute(up, "tp", ups), lax.ppermute(down, "tp", downs)


def line_owners():
    place = lax.axis_index("tp")
    first = jnp.where(place == 0, 1, place - 1)
    second = jnp.where(place == 0, 2, jnp.where(place == 3, 1, place + 1))
    third = jnp.where(place < 2, 3, 0)
    pick_second = jnp.where(place == 0, 1, jnp.where(place == 3, 2, 0))
    outer = (place == 0) | (place == 3)
    return [(place, 0 * place), (first, place == 0), (second, pick_second), (third, outer)]


def gather_line(value, work):
    up1, down1 = line_hop(value, value, [(0, 1), (1, 2), (2, 3)], [(3, 2), (2, 1), (1, 0)])
    work(0, [value])
    up2, down2 = line_hop(up1, down1, [(1, 2), (2, 3)], [(2, 1), (1, 0)])
    work(1, [up1, down1])
    inner = jnp.where(lax.axis_index("tp") == 2, up2, down2)
    outer = lax.ppermute(inner, "tp", [(2, 3), (1, 0)])
    work(2, [down1, down2, up2])
    work(3, [inner, outer])


OWNER, PICK, COLUMN, CHIP, CORE, LAST = 0, 4, 8, 12, 13, 14


def project_kernel(step, count, facts_ref, *refs):
    refs = list(refs)
    shards = refs[:count]
    mean_ref, rstd_ref, gain_ref, w_ref = refs[count : count + 4]
    del refs[: count + 4]
    previous_ref = refs.pop(0) if step > 0 else None
    kind = pl.program_id(0)
    normed_ref, turned_ref = refs[-2:]

    for pick, x_ref in enumerate(shards):

        @pl.when((kind == 0) & (facts_ref[PICK + step] == pick))
        def _():
            centred = x_ref[...].astype(jnp.float32) - mean_ref[...]
            normed_ref[...] = (centred * rstd_ref[...] * gain_ref[0]).astype(jnp.bfloat16)

    total = jnp.dot(normed_ref[...], w_ref[0], preferred_element_type=jnp.float32)
    if step > 0:
        total = total + previous_ref[0]
    if step < 3:
        refs[0][0] = total
        return
    cos_ref, sin_ref = refs[:2]
    kept_refs, given_ref = refs[5:9], refs[9]
    chip, core = facts_ref[CHIP], facts_ref[CORE]
    turned = total.T * jnp.where(kind == 0, QUERY_SCALE, 1.0)
    turned_ref[...] = turned.reshape(turned_ref.shape).astype(jnp.bfloat16)

    @pl.when(kind < 2)
    def _():
        half = ROT // 2
        for head in range(turned_ref.shape[0]):
            part = turned[head * HD : head * HD + ROT]
            swapped = jnp.concatenate([part[half:], part[:half]], axis=0)
            rotated = part * cos_ref[...] + swapped * sin_ref[...]
            rest = turned[head * HD + ROT : head * HD + 32]
            turned_ref[head, :32] = jnp.concatenate([rotated, rest], axis=0).astype(jnp.bfloat16)

    for distance in range(4):
        head = 2 * (chip ^ distance)
        kept_refs[distance][...] = turned_ref[head + core]
        given_ref[distance] = turned_ref[head + 1 - core]


def project(step, facts, shards, mean, rstd, gain, w3, previous, tables, waited):
    rows, depth = shards[0].shape
    width = w3.shape[2]
    column = pl.BlockSpec((rows, 1), lambda c, o: (0, 0))
    in_specs = [pl.BlockSpec((rows, depth), lambda c, o: (0, 0)) for _ in shards] + [
        column,
        column,
        pl.BlockSpec((1, 1, depth), lambda c, o: (o[OWNER + step], 0, 0)),
        pl.BlockSpec((1, depth, width), lambda c, o: (c, o[OWNER + step], 0)),
    ]
    args = [*shards, mean, rstd, gain, w3]
    sums = pl.BlockSpec((1, rows, width), lambda c, o: (c, 0, 0))
    if step > 0:
        in_specs.append(sums)
        args.append(previous)
    out_shape, out_specs = jax.ShapeDtypeStruct((3, rows, width), jnp.float32), sums
    if step == 3:
        in_specs += [pl.BlockSpec((ROT, rows), lambda c, o: (0, 0))] * 2
        in_specs += [pl.BlockSpec(memory_space=pl.ANY)] * len(waited)
        args += tables + waited
        out_shape = [jax.ShapeDtypeStruct((3 * HD, rows), jnp.bfloat16)] * 4
        out_shape.append(jax.ShapeDtypeStruct((4, 3 * HD, rows), jnp.bfloat16))
        out_specs = [pl.BlockSpec((HD, rows), lambda c, o: (c, 0))] * 4
        out_specs.append(pl.BlockSpec((4, HD, rows), lambda c, o: (0, c, 0)))
    return pl.pallas_call(
        functools.partial(project_kernel, step, len(shards)),
        grid_spec=pltpu.PrefetchScalarGridSpec(
            num_scalar_prefetch=1,
            grid=(3,),
            in_specs=in_specs,
            out_specs=out_specs,
            scratch_shapes=[
                pltpu.VMEM((rows, depth), jnp.bfloat16),
                pltpu.VMEM((width // HD, HD, rows), jnp.bfloat16),
            ],
        ),
        out_shape=out_shape,
        compiler_params=pltpu.CompilerParams(vmem_limit_bytes=48 << 20),
        cost_estimate=pl.CostEstimate(
            flops=(1, 20, 20, 6)[step] * rows * depth * width, bytes_accessed=0, transcendentals=0
        ),
        name="project",
    )(facts, *args)


def attend_kernel(facts_ref, pair_ref, start_ref, *refs):
    pieces, outs, (q_ref, k_ref, v_ref, top_ref, sum_ref, acc_ref) = refs[:-10], refs[-10:-6], refs[-6:]
    chip, own_core = facts_ref[CHIP], facts_ref[CORE]
    rows = q_ref.shape[2]
    for distance in range(4):
        for other, piece in enumerate(pieces[2 * distance : 2 * distance + 2]):
            block = 2 * (chip ^ distance) + (own_core ^ other)
            q_ref[block] = piece[:HD]
            k_ref[block] = piece[HD : 2 * HD].T
            v_ref[block] = piece[2 * HD :]
    def one_block(block, carry):
        token = block * rows + lax.broadcasted_iota(jnp.int32, (1, rows), 1)
        start = start_ref[block]
        top_ref[...] = jnp.full_like(top_ref, -1e30)
        sum_ref[...] = jnp.zeros_like(sum_ref)
        acc_ref[...] = jnp.zeros_like(acc_ref)

        def update(other, masked):
            scores = jnp.dot(k_ref[other], q_ref[block], preferred_element_type=jnp.float32)
            if masked:
                key = other * rows + lax.broadcasted_iota(jnp.int32, (rows, rows), 0)
                scores = jnp.where((key >= start) & (key <= token), scores, -jnp.inf)
            newest = jnp.maximum(top_ref[...], jnp.max(scores, axis=0, keepdims=True))
            shrink = jnp.exp2(top_ref[...] - newest)
            weights = jnp.exp2(scores - newest)
            top_ref[...] = newest
            sum_ref[...] = sum_ref[...] * shrink + jnp.sum(weights, axis=0, keepdims=True)
            acc_ref[...] = acc_ref[...] * shrink + jnp.dot(
                v_ref[other], weights.astype(jnp.bfloat16), preferred_element_type=jnp.float32
            )

        def one_pair(other, inner):
            live = pair_ref[block, other] > 0
            whole = facts_ref[LAST + block] <= other * rows

            @pl.when(live & whole & (other < block))
            def _():
                update(other, False)

            @pl.when(live & ~(whole & (other < block)))
            def _():
                update(other, True)

            return inner

        lax.fori_loop(0, block + 1, one_pair, 0)
        mixed = (acc_ref[...] / sum_ref[...]).astype(jnp.bfloat16)
        for distance, out_ref in enumerate(outs):

            @pl.when((block // 2) ^ chip == distance)
            def _():
                out_ref[block % 2] = mixed

        return carry

    lax.fori_loop(0, q_ref.shape[0], one_block, 0)


def attend(facts, pair_table, start, pieces):
    blocks, _, rows = start.shape
    smem = pl.BlockSpec(memory_space=pltpu.SMEM)
    vmem = pl.BlockSpec(memory_space=pltpu.VMEM)
    return pl.pallas_call(
        attend_kernel,
        in_specs=[smem, smem, vmem] + [vmem] * len(pieces),
        out_specs=[vmem] * 4,
        out_shape=[jax.ShapeDtypeStruct((2, HD, rows), jnp.bfloat16)] * 4,
        scratch_shapes=[
            pltpu.VMEM((blocks, HD, rows), jnp.bfloat16),
            pltpu.VMEM((blocks, rows, HD), jnp.bfloat16),
            pltpu.VMEM((blocks, HD, rows), jnp.bfloat16),
            pltpu.VMEM((1, rows), jnp.float32),
            pltpu.VMEM((1, rows), jnp.float32),
            pltpu.VMEM((HD, rows), jnp.float32),
        ],
        compiler_params=pltpu.CompilerParams(vmem_limit_bytes=28 << 20),
        cost_estimate=pl.CostEstimate(flops=1000, bytes_accessed=1000, transcendentals=0),
        name="attend",
    )(facts, pair_table, start, *pieces)


def swap(value, distance):
    count = lax.axis_size("blk")
    return lax.ppermute(value, "blk", [(place, place ^ distance) for place in range(count)])


def to_heads(kept, got):
    pieces = []
    for distance in range(4):
        for value in (kept[distance], got[distance]):
            pieces.append(value if distance == 0 else swap(value, 2 * distance))
    return pieces


def order_kernel(facts_ref, *refs):
    pairs, got_ref, out_ref = refs[:4], refs[4], refs[5]
    chip, core = facts_ref[CHIP], facts_ref[CORE]
    for distance in range(4):
        head = 2 * (chip ^ distance)
        out_ref[head + core] = pairs[distance][core]
        out_ref[head + 1 - core] = got_ref[distance]


def to_blocks(facts, mixed):
    core = lax.axis_index("blk") % 2
    held = mixed[:1] + [swap(mixed[distance], 2 * distance) for distance in (1, 2, 3)]
    given = [lax.dynamic_index_in_dim(pair, 1 - core, 0, keepdims=False) for pair in held]
    got = swap(jnp.stack(given), 1)
    vmem = pl.BlockSpec(memory_space=pltpu.VMEM)
    heads = pl.pallas_call(
        order_kernel,
        in_specs=[pl.BlockSpec(memory_space=pltpu.SMEM)] + [vmem] * 5,
        out_specs=vmem,
        out_shape=jax.ShapeDtypeStruct((8,) + got.shape[1:], got.dtype),
        cost_estimate=pl.CostEstimate(flops=0, bytes_accessed=2 << 20, transcendentals=0),
        name="order",
    )(facts, *held, got)
    return heads.reshape((8 * HD,) + got.shape[2:])


def combine_kernel(steps, counts, facts_ref, *refs):
    refs = list(refs)
    arrays = []
    for count in counts:
        arrays.append(refs[:count])
        del refs[:count]
    own_ref, others_ref = (refs.pop(0) if 0 in steps else None), refs.pop(0)
    previous_ref = refs.pop(0) if 0 not in steps else None
    out_ref, sum_ref = refs
    slot = pl.program_id(1)
    for place, step in enumerate(steps):
        for pick, h_ref in enumerate(arrays[place]):

            @pl.when((slot == place) & (facts_ref[PICK + step] == pick))
            def _():
                w_ref = own_ref if step == 0 else others_ref
                product = lax.dot_general(
                    h_ref[...],
                    w_ref[...].reshape(h_ref.shape[0], out_ref.shape[1]),
                    (((0,), (0,)), ((), ())),
                    preferred_element_type=jnp.float32,
                )
                if place > 0:
                    product = product + sum_ref[...]
                elif previous_ref is not None:
                    product = product + previous_ref[...].astype(jnp.float32)
                if place < len(steps) - 1:
                    sum_ref[...] = product
                else:
                    out_ref[...] = product.astype(out_ref.dtype)


def combine(steps, facts, arrays, own, others, previous=None):
    depth, rows = arrays[-1][-1].shape
    outer, _, inner, width = others.shape
    tile = width // 2
    out_spec = pl.BlockSpec((rows, tile), lambda n, k, o: (0, n))
    in_specs = [pl.BlockSpec((depth, rows), lambda n, k, o: (0, 0)) for step in arrays for _ in step]
    args = [array for step in arrays for array in step]
    if 0 in steps:
        in_specs.append(
            pl.BlockSpec((depth, tile), lambda n, k, o: (0, o[OWNER] * (width // tile) + n))
        )
        args.append(own)
    in_specs.append(
        pl.BlockSpec((outer, 1, inner, tile), lambda n, k, o: (0, o[COLUMN + steps[0] + k], 0, n))
    )
    args.append(others)
    if 0 not in steps:
        in_specs.append(out_spec)
        args.append(previous)
    return pl.pallas_call(
        functools.partial(combine_kernel, steps, tuple(len(step) for step in arrays)),
        grid_spec=pltpu.PrefetchScalarGridSpec(
            num_scalar_prefetch=1,
            grid=(width // tile, len(steps)),
            in_specs=in_specs,
            out_specs=out_spec,
            scratch_shapes=[pltpu.VMEM((rows, tile), jnp.float32)],
        ),
        out_shape=jax.ShapeDtypeStruct((rows, width), jnp.bfloat16),
        compiler_params=pltpu.CompilerParams(vmem_limit_bytes=56 << 20),
        cost_estimate=pl.CostEstimate(
            flops=4 * len(steps) * rows * depth * width,
            bytes_accessed=2 * len(steps) * depth * width,
            transcendentals=0,
        ),
        name="combine",
    )(facts, *args)


def share_kernel(facts_ref, w_ref, *refs):
    outs, sems = refs[:3], refs[3]
    rows, width = outs[0].shape
    first = facts_ref[0] * rows
    copies = []
    for place, out_ref in enumerate(outs):
        begin = pl.multiple_of(facts_ref[1 + place] * width, width)
        window = w_ref.at[pl.ds(pl.multiple_of(first, rows), rows), pl.ds(begin, width)]
        copies.append(pltpu.make_async_copy(window, out_ref, sems.at[place]))
    for copy in copies:
        copy.start()
    for copy in copies:
        copy.wait()


def shares(numbers, w_out, width):
    any_space = pl.BlockSpec(memory_space=pl.ANY)
    return pl.pallas_call(
        share_kernel,
        in_specs=[pl.BlockSpec(memory_space=pltpu.SMEM), any_space],
        out_specs=[pl.BlockSpec(memory_space=pltpu.VMEM)] * 3,
        out_shape=[jax.ShapeDtypeStruct((HD, width), w_out.dtype)] * 3,
        scratch_shapes=[pltpu.SemaphoreType.DMA((3,))],
        cost_estimate=pl.CostEstimate(flops=0, bytes_accessed=2 << 20, transcendentals=0),
        name="shares",
    )(numbers, w_out)


def stack_kernel(*refs):
    for place in range(3):
        refs[-1][place] = refs[place][...]


def stack(values, waited):
    any_space, vmem = pl.BlockSpec(memory_space=pl.ANY), pl.BlockSpec(memory_space=pltpu.VMEM)
    return pl.pallas_call(
        stack_kernel,
        in_specs=[vmem] * 3 + [any_space] * len(waited),
        out_specs=vmem,
        out_shape=jax.ShapeDtypeStruct((3,) + values[0].shape, values[0].dtype),
        cost_estimate=pl.CostEstimate(flops=0, bytes_accessed=2 << 20, transcendentals=0),
        name="stack",
    )(*values, *waited)


def pages_kernel(facts_ref, *refs):
    kept_refs, given_ref, out_ref, turned_ref = refs[:4], refs[4], refs[5], refs[6]
    blocks = facts_ref.shape[0] - LAST - out_ref.shape[1]
    chip, core = facts_ref[CHIP], facts_ref[CORE]
    for tile in range(given_ref.shape[2] // 128):
        tokens = slice(tile * 128, (tile + 1) * 128)
        for kind in range(2):
            entries = slice((kind + 1) * HD, (kind + 2) * HD)
            for distance in range(4):
                head = 2 * (chip ^ distance)
                turned_ref[head + core] = kept_refs[distance][entries, tokens]
                turned_ref[head + 1 - core] = given_ref[distance, entries, tokens]
            turned = turned_ref[...].reshape(8 * HD, 128).T
            for page in range(128 // PAGE):
                place = facts_ref[LAST + blocks + tile * 128 // PAGE + page]
                out_ref[kind, place] = turned[page * PAGE : (page + 1) * PAGE]


def pages(facts, count, parts):
    width = 8 * HD
    vmem = pl.BlockSpec(memory_space=pltpu.VMEM)
    return pl.pallas_call(
        pages_kernel,
        in_specs=[pl.BlockSpec(memory_space=pltpu.SMEM)] + [vmem] * len(parts),
        out_specs=vmem,
        scratch_shapes=[pltpu.VMEM((8, HD, 128), jnp.bfloat16)],
        out_shape=jax.ShapeDtypeStruct((2, count, PAGE, width), jnp.bfloat16),
        compiler_params=pltpu.CompilerParams(vmem_limit_bytes=56 << 20),
        cost_estimate=pl.CostEstimate(flops=0, bytes_accessed=10 << 20, transcendentals=0),
        name="pages",
    )(facts, *parts)


def per_device_heads(hidden_in, ln_gain, w_qkv, w_out, doc_lengths, segment_ids, pair_table, page_table):
    rows, depth = hidden_in.shape
    width = w_qkv.shape[2]
    block, place = lax.axis_index("blk"), lax.axis_index("tp")
    chip = block // 2
    blocks = lax.axis_size("blk")
    values32 = hidden_in.astype(jnp.float32)
    own_mean = jnp.mean(values32, axis=1)
    own_square = jnp.mean((values32 - own_mean[:, None]) ** 2, axis=1)
    own_stats = jnp.stack([own_mean, own_square])
    stats = jnp.stack([own_stats] + [turn(own_stats, distance) for distance in (1, 2, 3)])
    mean = jnp.mean(stats[:, 0], axis=0)
    variance = jnp.mean(stats[:, 1] + (stats[:, 0] - mean[None]) ** 2, axis=0)
    rstd = lax.rsqrt(variance + EPSILON)[:, None]
    mean = mean[:, None]
    gain = ln_gain.reshape(4, 1, depth)
    w3 = jnp.transpose(w_qkv, (1, 0, 2))

    token_index = block * rows + jnp.arange(rows, dtype=jnp.int32)
    positions = doc_positions(token_index, doc_lengths, segment_ids)
    frequency = 10000.0 ** (-(2.0 * jnp.arange(ROT // 2, dtype=jnp.float32)) / ROT)
    angles = positions.astype(jnp.float32)[None, :] * frequency[:, None]
    cosine, sine = jnp.cos(angles), jnp.sin(angles)
    cosine = jnp.concatenate([cosine, cosine])
    sine = jnp.concatenate([-sine, sine])

    ends = jnp.cumsum(doc_lengths)
    tokens = jnp.arange(blocks * rows, dtype=jnp.int32)
    start = jnp.max(jnp.where(ends[:, None] <= tokens[None, :], ends[:, None], 0), axis=0)
    start = start.astype(jnp.int32).reshape(blocks, 1, rows)
    page_count = rows // PAGE
    steps = line_owners()
    numbers = [owner for owner, _ in steps] + [pick for _, pick in steps]
    numbers += [jnp.maximum((place - owner) % 4 - 1, 0) for owner, _ in steps] + [chip, block % 2]
    facts = jnp.concatenate(
        [
            jnp.stack([jnp.asarray(number).astype(jnp.int32) for number in numbers]),
            start[:, 0, rows - 1],
            page_table - block * page_count,
        ]
    )

    windows = jnp.stack([block] + [(place + distance) % 4 for distance in (1, 2, 3)]).astype(jnp.int32)
    windows = shares(windows, w_out, depth)
    windows = list(windows)
    total = [None]

    def take_in(step, arrays):
        total[0] = project(
            step, facts, arrays, mean, rstd, gain, w3, total[0], [cosine, sine], windows
        )

    gather_line(hidden_in, take_in)
    *kept, given = total[0]
    arrived = to_heads(kept, swap(given, 1))
    page_cache = pages(facts, page_count, [*kept, given])

    columns = [turn(window, distance) for distance, window in zip((1, 2, 3), windows)]
    mixed = list(attend(facts, pair_table, start, arrived))
    others = lax.all_gather(stack(columns, mixed[:1]), "blk", axis=0)
    heads = to_blocks(facts, mixed)

    came, result = [], [None]

    def add_in(step, arrays):
        came.append(arrays)
        if step == 2:
            result[0] = combine((0, 1, 2), facts, came[:3], w_out, others)
        if step == 3:
            result[0] = combine((3,), facts, came[3:], None, others, result[0])

    gather_line(heads, add_in)
    attn_out = result[0]
    return (attn_out, page_cache)


def solution(mesh):
    placed = (P("blk", "tp"), P(), P(None, None, "tp"), P("tp", None), P(), P("blk"), P(), P("blk"))

    def per_device(hidden_in, ln_gain, w_qkv, *rest):
        heads = w_qkv.shape[2] // HD
        fits = mesh.shape["tp"] == 4 and mesh.shape["blk"] == 8 and heads == 8
        form = per_device_heads if fits else per_device_any
        return form(hidden_in, ln_gain, w_qkv, *rest)

    return jax.shard_map(
        per_device,
        mesh=mesh,
        in_specs=placed,
        out_specs=(P("blk", "tp"), P(None, "blk", None, "tp")),
        check_vma=False,
    )
```
